32 devices in a mesh: dp: 16 (over z, y, x), tensor: 2 (over core).
Axes of the slice: x: 2, y: 2, z: 4, core: 2. Of those that a mesh axis runs over, the one named last changes fastest.
Arguments:
- tokens: float32 [6144, 768], P('dp'), may hold values from -6 to 6
- cotangent: float32 [6144, 768], P('dp'), may hold values from -6 to 6
- doc_ids: int32 [16, 384], P('dp'), may hold values from 0 to 3, never falling along the last dimension, each value on 1 to 288 neighbouring positions
- live_rows: int32 [16], P('dp'), may hold values from 96 to 384, as said below
- ln1_gain: float32 [2, 768], replicated, may hold values from 0.1 to 1.9
- ln1_shift: float32 [2, 768], replicated, may hold values from -3 to 3
- qkv_weight: bfloat16 [2, 3, 768, 768], P(None, None, None, 'tensor'), may hold values from -0.21875 to 0.21875
- qv_bias: float32 [2, 2, 768], P(None, None, 'tensor'), may hold values from -3 to 3
- proj_weight: bfloat16 [2, 768, 768], P(None, 'tensor'), may hold values from -1.75 to 1.75
- proj_bias: float32 [2, 768], replicated, may hold values from -3 to 3
- ln2_gain: float32 [2, 768], replicated, may hold values from 0.1 to 1.9
- ln2_shift: float32 [2, 768], replicated, may hold values from -3 to 3
- fc_weight: bfloat16 [2, 768, 3072], P(None, None, 'tensor'), may hold values from -0.21875 to 0.21875
- fc_bias: float32 [2, 3072], P(None, 'tensor'), may hold values from -3 to 3
- out_weight: bfloat16 [2, 3072, 768], P(None, 'tensor'), may hold values from -0.21875 to 0.21875
- out_bias: float32 [2, 768], replicated, may hold values from -3 to 3
Outputs:
- block_out: float32 [6144, 768], P('dp')
- input_grad: float32 [6144, 768], P('dp')
- grad_ln1_gain: float32 [2, 768], replicated
- grad_ln1_shift: float32 [2, 768], replicated
- grad_qkv: float32 [2, 3, 768, 768], P(None, None, 'dp', 'tensor')
- grad_qv_bias: float32 [2, 2, 768], P(None, None, 'tensor')
- grad_proj: float32 [2, 768, 768], P(None, 'tensor', 'dp')
- grad_proj_bias: float32 [2, 768], replicated
- grad_ln2_gain: float32 [2, 768], replicated
- grad_ln2_shift: float32 [2, 768], replicated
- grad_fc: float32 [2, 768, 3072], P(None, 'dp', 'tensor')
- grad_fc_bias: float32 [2, 3072], P(None, 'tensor')
- grad_out: float32 [2, 3072, 768], P(None, 'tensor', 'dp')
- grad_out_bias: float32 [2, 768], replicated
The draws below stay inside these ranges and needn't reach their ends.
Inputs may be any that keep to these rules, and one draw needn't show every extreme that they name: `live_rows`: some index of dp has all 384 rows live in every draw; the others hold at least a quarter of them.
All inputs are finite; a program needn't handle non-finite values.
Results may differ from the reference program's by a relative error of at most 0.0003.
Values sent between devices are 32-bit elements; how exact they have to be, the bound alone decides.
No kernel may reach another device: no remote copies, remote signals or barrier semaphores. Data moves between devices by JAX's collectives and lax.ppermute only.
A program may use at most 192 MiB of HBM per device.

```python
import math
import jax
import jax.numpy as jnp
import numpy as np
from jax import lax

D = 768
HEADS = 12
FF = 3072
HEAD_DIM = 64
LAYERS = 2
SEGS = 4
TOK_DEV = 384
TOKENS = 6144
N_DP = 16


def draw_live_rows(key, part):
    key = jax.random.fold_in(key, 5)
    first_key, second_key = jax.random.split(key)
    counts = jax.random.randint(first_key, (N_DP,), TOK_DEV // 4, TOK_DEV + 1)
    chosen = jax.random.randint(second_key, (), 0, N_DP)
    return jnp.where(jnp.arange(N_DP) == chosen, TOK_DEV, counts).astype(jnp.int32)


def shard_levels(rng, shape, shards, low, top_value):
    gain, own = 1.0, jax.random.fold_in(rng, 6)
    for axis_at, blocks in shards:
        steps = jnp.exp(jax.random.uniform(jax.random.fold_in(own, axis_at), (blocks,), jnp.float32, low / len(shards), top_value / len(shards)))
        gain = gain * jnp.repeat(steps, shape[axis_at] // blocks).reshape([-1 if axis == axis_at else 1 for axis in range(len(shape))])
    return gain


def length_profile(count, total, reach, skew):
    portions = [(1 << 20) // math.isqrt(standing ** skew) + 1 for standing in range(2, count + 1)]
    surplus, holding = total - reach - (count - 1), [1] * (count - 1)
    while surplus > 0:
        free = [i for i in range(count - 1) if holding[i] < reach]
        pool, remaining = sum([portions[i] for i in free]), surplus
        for i in free:
            more = min(reach - holding[i], max(1, remaining * portions[i] // pool), surplus)
            holding[i] = holding[i] + more
            surplus = surplus - more
    return np.array([reach] + holding)


def uneven_parts(key, number_of, total, most, lean):
    if number_of == 2:
        one = jax.random.randint(key, (), max(1, total - most), min(most, total - 1) + 1)
        return jnp.stack([one, total - one])
    lengths = jnp.asarray(length_profile(number_of, total, most, lean), jnp.int32)
    pairs = (number_of - 1) // 2
    source_of, taker = lengths[1:1 + 2 * pairs:2], lengths[2:2 + 2 * pairs:2]
    room = jnp.minimum(source_of - 1, most - taker)
    shifted = jax.random.randint(jax.random.fold_in(key, 1), (pairs,), 0, 1 << 20) % (room + 1)
    lengths = lengths.at[1:1 + 2 * pairs:2].set(source_of - shifted).at[2:2 + 2 * pairs:2].set(taker + shifted)
    return lengths[jax.random.permutation(jax.random.fold_in(key, 2), number_of)]


def bell_draw(key, dims, spread, bound, cuts=(), held_as=jnp.bfloat16):
    entries = jax.random.normal(key, dims, jnp.float32) * spread
    if len(cuts) > 0:
        entries = shard_levels(key, dims, cuts, -0.22, 0.18) * entries
    return jnp.clip(entries, min=-bound, max=bound).astype(held_as)


def setup_inputs(seed: int = 0) -> dict:
    arg_keys = jax.random.split(jax.random.key(seed), 17)
    tokens = bell_draw(arg_keys[0], (TOKENS, D), 1.0, 6.0, ((0, 16),), jnp.float32)
    cotangent = bell_draw(arg_keys[1], (TOKENS, D), 1.0, 6.0, ((0, 16),), jnp.float32)
    doc_ids = jax.vmap(lambda own: jnp.searchsorted(jnp.cumsum(uneven_parts(own, SEGS, TOK_DEV, TOK_DEV * 3 // 4, 1)), jnp.arange(TOK_DEV), side="right"))(jax.random.split(arg_keys[2], N_DP)).reshape((N_DP, TOK_DEV)).astype(jnp.int32)
    live_rows = draw_live_rows(jax.random.fold_in(arg_keys[16], 71), 0)
    ln1_gain = jnp.clip(1.0 + 0.18 * jax.random.normal(arg_keys[4], (LAYERS, D), jnp.float32), 0.1, 1.9)
    ln1_shift = bell_draw(arg_keys[5], (LAYERS, D), 0.5, 3.0, (), jnp.float32)
    qkv_weight = bell_draw(arg_keys[6], (LAYERS, 3, D, D), D ** -0.5, 0.21875, ((3, 2),))
    qv_bias = bell_draw(arg_keys[7], (LAYERS, 2, D), 0.5, 3.0, ((2, 2),), jnp.float32)
    proj_weight = bell_draw(arg_keys[8], (LAYERS, D, D), (D // 64) ** -0.5, 1.75, ((1, 2),))
    proj_bias = bell_draw(arg_keys[9], (LAYERS, D), 0.5, 3.0, (), jnp.float32)
    ln2_gain = jnp.clip(1.0 + 0.18 * jax.random.normal(arg_keys[10], (LAYERS, D), jnp.float32), 0.1, 1.9)
    ln2_shift = bell_draw(arg_keys[11], (LAYERS, D), 0.5, 3.0, (), jnp.float32)
    fc_weight = bell_draw(arg_keys[12], (LAYERS, D, FF), D ** -0.5, 0.21875, ((2, 2),))
    fc_bias = bell_draw(arg_keys[13], (LAYERS, FF), 0.5, 3.0, ((1, 2),), jnp.float32)
    out_weight = bell_draw(arg_keys[14], (LAYERS, FF, D), (FF // 4) ** -0.5, 0.21875, ((1, 2),))
    out_bias = bell_draw(arg_keys[15], (LAYERS, D), 0.5, 3.0, (), jnp.float32)
    return {"tokens": tokens, "cotangent": cotangent, "doc_ids": doc_ids, "live_rows": live_rows, "ln1_gain": ln1_gain, "ln1_shift": ln1_shift, "qkv_weight": qkv_weight, "qv_bias": qv_bias, "proj_weight": proj_weight, "proj_bias": proj_bias, "ln2_gain": ln2_gain, "ln2_shift": ln2_shift, "fc_weight": fc_weight, "fc_bias": fc_bias, "out_weight": out_weight, "out_bias": out_bias}


@jax.custom_vjp
def low(v):
    return lax.optimization_barrier(v.astype(jnp.bfloat16)).astype(jnp.float32)

@jax.custom_vjp
def low_back(v):
    return v

def low_keep(v):
    return (low(v), None)

def low_pass(kept, grad):
    return (grad,)

def back_keep(v):
    return (v, None)

def back_low(kept, grad):
    return (low(grad),)
low.defvjp(low_keep, low_pass)
low_back.defvjp(back_keep, back_low)
EPSILON = 1e-05
HIGHEST = lax.Precision.HIGHEST

def matmul(operand, partner):
    return jnp.dot(operand, partner, precision=HIGHEST, preferred_element_type=jnp.float32)

def layer_norm(values, norm_gain, norm_shift):
    row_mean = lax.optimization_barrier(jnp.mean(values, axis=-1, keepdims=True))
    centred = values - row_mean
    variance = lax.optimization_barrier(jnp.mean(centred * centred, axis=-1, keepdims=True))
    return centred * lax.rsqrt(variance + EPSILON) * norm_gain + norm_shift

def attention(queries, key_rows, values, allowed):
    scores = jnp.einsum('qhe,khe->hqk', queries, key_rows, precision=HIGHEST) * HEAD_DIM ** (-0.5)
    scores = jnp.where(allowed[None], scores, jnp.float32(-1e+30))
    weights = jax.nn.softmax(scores, axis=-1)
    return jnp.einsum('hqk,khe->qhe', weights, values, precision=HIGHEST)

def one_group(params, rows_in, docs, living_count):
    ln1_gain, ln1_shift, qkv_weight, qv_bias, proj_weight, proj_bias, ln2_gain, ln2_shift, fc_weight, fc_bias, out_weight, out_bias = params
    row_count = rows_in.shape[0]
    position = jnp.arange(row_count, dtype=jnp.int32)
    living = position < living_count
    doc_tags = jnp.where(living, docs, -1)
    allowed = (doc_tags[:, None] == doc_tags[None, :]) & (position[None, :] <= position[:, None])
    head_shape = (row_count, HEADS, HEAD_DIM)
    stream = rows_in
    for number in range(LAYERS):
        normed = layer_norm(stream, ln1_gain[number], ln1_shift[number])
        queries = matmul(normed, qkv_weight[number, 0]) + qv_bias[number, 0]
        key_rows = matmul(normed, qkv_weight[number, 1])
        values = matmul(normed, qkv_weight[number, 2]) + qv_bias[number, 1]
        attended = attention(queries.reshape(head_shape), key_rows.reshape(head_shape), values.reshape(head_shape), allowed).reshape(row_count, D)
        middle = stream + matmul(attended, proj_weight[number]) + proj_bias[number]
        normed_two = layer_norm(middle, ln2_gain[number], ln2_shift[number])
        hidden_in = matmul(normed_two, fc_weight[number]) + fc_bias[number]
        activated = jax.nn.gelu(hidden_in, approximate=True)
        stream = middle + matmul(activated, out_weight[number]) + out_bias[number]
    return stream * living[:, None].astype(jnp.float32)

def reference(tokens, cotangent, doc_ids, live_rows, ln1_gain, ln1_shift, qkv_weight, qv_bias, proj_weight, proj_bias, ln2_gain, ln2_shift, fc_weight, fc_bias, out_weight, out_bias):
    params = (ln1_gain, ln1_shift, qkv_weight.astype(jnp.float32), qv_bias, proj_weight.astype(jnp.float32), proj_bias, ln2_gain, ln2_shift, fc_weight.astype(jnp.float32), fc_bias, out_weight.astype(jnp.float32), out_bias)
    grouped = tokens.reshape(N_DP, TOK_DEV, D)
    cot_grouped = cotangent.reshape(N_DP, TOK_DEV, D)

    def forward(param_set, rows_all):
        step_fn = jax.checkpoint(lambda item: one_group(param_set, item[0], item[1], item[2]))
        return lax.map(step_fn, (rows_all, doc_ids, live_rows))
    outputs, pull_back = jax.vjp(forward, params, grouped)
    param_grads, rows_grad = pull_back(cot_grouped)
    return (outputs.reshape(TOKENS, D), rows_grad.reshape(TOKENS, D), param_grads[0], param_grads[1], param_grads[2], param_grads[3], param_grads[4], param_grads[5], param_grads[6], param_grads[7], param_grads[8], param_grads[9], param_grads[10], param_grads[11])
```

```python
import functools

import jax
import jax.numpy as jnp
from jax import lax
from jax.experimental import pallas as pl
from jax.experimental.pallas import tpu as pltpu
from jax.sharding import PartitionSpec as P

HEAD_DIM = 64
EPSILON = 1e-05
HIGH = lax.Precision.HIGH
LANES = 128
F32 = jnp.float32
BF16 = jnp.bfloat16


def split_two(values):
    high = lax.reduce_precision(values, 8, 7)
    return high.astype(BF16), (values - high).astype(BF16)


def weight_product(values, weight, contract):
    high, low = split_two(values)
    dims = (((1,), (contract,)), ((), ()))
    first = lax.dot_general(high, weight, dims, preferred_element_type=F32)
    return first + lax.dot_general(low, weight, dims, preferred_element_type=F32)


def pair_sum(values, pairs):
    return values + lax.ppermute(values, "tensor", pairs)


def norm_forward(values, norm_gain, norm_shift):
    centred = values - jnp.mean(values, axis=-1, keepdims=True)
    scale = lax.rsqrt(jnp.mean(centred * centred, axis=-1, keepdims=True) + EPSILON)
    unit = centred * scale
    return unit * norm_gain + norm_shift, unit, scale


def norm_backward(grad, unit, scale, norm_gain):
    gained = grad * norm_gain
    mean_grad = jnp.mean(gained, axis=-1, keepdims=True)
    mean_dot = jnp.mean(gained * unit, axis=-1, keepdims=True)
    return (
        scale * (gained - mean_grad - unit * mean_dot),
        jnp.sum(grad * unit, axis=0),
        jnp.sum(grad, axis=0),
    )


GELU_A = 0.7978845608028654
GELU_B = 0.044715


def gelu_forward(values):
    bent = jnp.tanh(GELU_A * (values + GELU_B * values * values * values))
    return 0.5 * values * (1.0 + bent)


def gelu_slope(values):
    square = values * values
    bent = jnp.tanh(GELU_A * (values + GELU_B * values * square))
    inner = GELU_A * (1.0 + 3.0 * GELU_B * square)
    return 0.5 * (1.0 + bent) + 0.5 * values * (1.0 - bent * bent) * inner


def masked_scores(queries, key_rows, allowed, score_scale):
    scores = jnp.einsum("qhe,khe->hqk", queries, key_rows, precision=HIGH) * score_scale
    return jnp.where(allowed[None], scores, jnp.float32(-1e30))


def attend(queries, key_rows, values, allowed, score_scale):
    scores = masked_scores(queries, key_rows, allowed, score_scale)
    row_peak = jnp.max(scores, axis=-1, keepdims=True)
    row_total = jnp.sum(jnp.exp(scores - row_peak), axis=-1, keepdims=True)
    logsum = row_peak + jnp.log(row_total)
    weights = jnp.exp(scores - logsum)
    return jnp.einsum("hqk,khe->qhe", weights, values, precision=HIGH), logsum


def attend_back(queries, key_rows, values, allowed, score_scale, logsum, result, result_grad):
    weights = jnp.exp(masked_scores(queries, key_rows, allowed, score_scale) - logsum)
    values_grad = jnp.einsum("hqk,qhe->khe", weights, result_grad, precision=HIGH)
    weights_grad = jnp.einsum("qhe,khe->hqk", result_grad, values, precision=HIGH)
    row_dot = jnp.sum(result_grad * result, axis=-1)
    scores_grad = weights * (weights_grad - jnp.transpose(row_dot)[:, :, None]) * score_scale
    query_grad = jnp.einsum("hqk,khe->qhe", scores_grad, key_rows, precision=HIGH)
    key_grad = jnp.einsum("hqk,qhe->khe", scores_grad, queries, precision=HIGH)
    return query_grad, key_grad, values_grad


def bit_orders(count):
    bits = [1 << at for at in range(count.bit_length() - 1)]
    lead, rest = bits[:3], bits[3:]
    return [lead[at:] + lead[:at] + rest for at in range(len(lead))]


def block_masks(order):
    masks = [0]
    for bit in reversed(order):
        masks = masks + [mask + bit for mask in masks]
    return masks


def grad_kernel(orders, widths, permuted, me_ref, a_ref, b_ref, *refs):
    outs = refs[: 2 * len(orders)]
    turned_high, turned_low, high_ref, low_ref = refs[2 * len(orders):]
    depth = high_ref.shape[0]
    half = depth // 2
    if not permuted:
        turned = a_ref[...].T
        high = turned.astype(BF16)
        turned_high[...] = high
        turned_low[...] = (turned - high.astype(F32)).astype(BF16)
    start = 0
    for number, order in enumerate(orders):
        masks = block_masks(order)
        if permuted:
            turned = a_ref[number]
            high = turned.astype(BF16)
            high_ref[...] = high
            low_ref[...] = (turned - high.astype(F32)).astype(BF16)
        else:
            rows = depth // len(masks)
            for place, mask in enumerate(masks):
                source = pl.ds(pl.multiple_of((me_ref[0] ^ mask) * rows, 16), rows)
                target = pl.ds(place * rows, rows)
                high_ref[target, :] = turned_high[source, :]
                low_ref[target, :] = turned_low[source, :]
        part = b_ref[:, start:start + widths[number]]
        part_high = part.astype(BF16)
        part_low = (part - part_high.astype(F32)).astype(BF16)
        for which in (1, 0):
            rows_at = pl.ds(which * half, half)
            out_ref = outs[2 * number + 1 - which]
            out_ref[...] = (
                jnp.dot(high_ref[rows_at, :], part_high, preferred_element_type=F32)
                + jnp.dot(high_ref[rows_at, :], part_low, preferred_element_type=F32)
                + jnp.dot(low_ref[rows_at, :], part_high, preferred_element_type=F32)
            )
        start += widths[number]


def grad_parts(left, right, me, count):
    orders = bit_orders(count)
    depth, columns = left.shape[1], right.shape[1]
    widths = flow_widths(columns)
    rows = depth // count
    permuted = rows % 16 != 0
    if permuted:
        blocks = left.T.reshape(count, rows, left.shape[0])
        left = jnp.stack(
            [
                jnp.take(blocks, me ^ jnp.array(block_masks(order), jnp.int32), axis=0).reshape(depth, -1)
                for order in orders
            ]
        )
    tokens = right.shape[0]
    shapes = []
    for width in widths:
        shapes += [jax.ShapeDtypeStruct((depth // 2, width), F32)] * 2
    outs = pl.pallas_call(
        functools.partial(grad_kernel, orders, widths, permuted),
        out_shape=shapes,
        in_specs=[pl.BlockSpec(memory_space=pltpu.SMEM)] + [pl.BlockSpec(memory_space=pltpu.VMEM)] * 2,
        out_specs=[pl.BlockSpec(memory_space=pltpu.VMEM)] * len(shapes),
        scratch_shapes=[pltpu.VMEM((depth, tokens), BF16)] * 4,
        compiler_params=pltpu.CompilerParams(vmem_limit_bytes=40 * 2**20),
        cost_estimate=pl.CostEstimate(
            flops=6 * depth * tokens * columns,
            bytes_accessed=4 * (depth * tokens + tokens * columns + depth * columns),
            transcendentals=0,
        ),
    )(me.reshape(1), left, right)
    return [(outs[2 * at], outs[2 * at + 1]) for at in range(len(orders))]


def flow_widths(columns):
    tiles = columns // LANES
    return {
        12: (6 * LANES, 4 * LANES, 2 * LANES),
        9: (4 * LANES, 3 * LANES, 2 * LANES),
        3: (LANES, LANES, LANES),
    }[tiles]


def scatter(parts, count):
    orders = bit_orders(count)
    done = []
    for (send, keep), order in zip(parts, orders):
        for at, bit in enumerate(order):
            got = lax.ppermute(send, "dp", [(one, one ^ bit) for one in range(count)])
            if at + 1 < len(order):
                half = keep.shape[0] // 2
                send = keep[half:] + got[half:]
                keep = keep[:half] + got[:half]
            else:
                keep = keep + got
        done.append(keep)
    return jnp.concatenate(done, axis=1)


def small_sum(values, count):
    bit = 1
    while bit < count:
        values = values + lax.ppermute(values, "dp", [(one, one ^ bit) for one in range(count)])
        bit *= 2
    return values


def on_device(
    count,
    pair,
    tokens,
    cotangent,
    doc_ids,
    live_rows,
    ln1_gain,
    ln1_shift,
    qkv_weight,
    qv_bias,
    proj_weight,
    proj_bias,
    ln2_gain,
    ln2_shift,
    fc_weight,
    fc_bias,
    out_weight,
    out_bias,
):
    row_count = tokens.shape[0]
    layer_count = qkv_weight.shape[0]
    local_heads = qkv_weight.shape[-1] // HEAD_DIM
    head_shape = (row_count, local_heads, HEAD_DIM)
    score_scale = HEAD_DIM ** (-0.5)
    pairs = [(one, one ^ 1) for one in range(pair)]
    me = lax.axis_index("dp").astype(jnp.int32)
    position = jnp.arange(row_count, dtype=jnp.int32)
    living = position < live_rows[0]
    doc_tags = jnp.where(living, doc_ids[0], -1)
    allowed = (doc_tags[:, None] == doc_tags[None, :]) & (position[None, :] <= position[:, None])
    live_mask = living[:, None].astype(F32)
    stored = []
    stream = tokens
    for number in range(layer_count):
        normed, unit, scale = norm_forward(stream, ln1_gain[number], ln1_shift[number])
        queries = (weight_product(normed, qkv_weight[number, 0], 0) + qv_bias[number, 0]).reshape(head_shape)
        key_rows = weight_product(normed, qkv_weight[number, 1], 0).reshape(head_shape)
        values = (weight_product(normed, qkv_weight[number, 2], 0) + qv_bias[number, 1]).reshape(head_shape)
        attended, logsum = attend(queries, key_rows, values, allowed, score_scale)
        attended_flat = attended.reshape(row_count, -1)
        branch = pair_sum(weight_product(attended_flat, proj_weight[number], 0), pairs)
        middle = stream + branch + proj_bias[number]
        normed_two, unit_two, scale_two = norm_forward(middle, ln2_gain[number], ln2_shift[number])
        hidden_in = weight_product(normed_two, fc_weight[number], 0) + fc_bias[number]
        activated = gelu_forward(hidden_in)
        branch = pair_sum(weight_product(activated, out_weight[number], 0), pairs)
        stream = middle + branch + out_bias[number]
        stored.append(
            (normed, unit, scale, queries, key_rows, values, attended, logsum, normed_two, unit_two, scale_two, hidden_in, activated)
        )
    block_out = stream * live_mask
    gradient = cotangent * live_mask
    small_terms = [None] * layer_count
    big_terms = [None] * layer_count
    for number in reversed(range(layer_count)):
        (normed, unit, scale, queries, key_rows, values, attended, logsum, normed_two, unit_two, scale_two, hidden_in, activated) = stored[number]
        attended_flat = attended.reshape(row_count, -1)
        grad_out_bias = jnp.sum(gradient, axis=0)
        grad_out = scatter(grad_parts(gradient, activated, me, count), count)
        hidden_grad = gelu_slope(hidden_in) * weight_product(gradient, out_weight[number], 1)
        grad_fc_bias = jnp.sum(hidden_grad, axis=0)
        grad_fc = scatter(grad_parts(normed_two, hidden_grad, me, count), count)
        normed_two_grad = pair_sum(weight_product(hidden_grad, fc_weight[number], 1), pairs)
        middle_grad, grad_ln2_gain, grad_ln2_shift = norm_backward(normed_two_grad, unit_two, scale_two, ln2_gain[number])
        gradient = gradient + middle_grad
        grad_proj_bias = jnp.sum(gradient, axis=0)
        grad_proj = scatter(grad_parts(gradient, attended_flat, me, count), count)
        attended_grad = weight_product(gradient, proj_weight[number], 1).reshape(head_shape)
        query_grad, key_grad, values_grad = attend_back(
            queries, key_rows, values, allowed, score_scale, logsum, attended, attended_grad
        )
        query_grad = query_grad.reshape(row_count, -1)
        key_grad = key_grad.reshape(row_count, -1)
        values_grad = values_grad.reshape(row_count, -1)
        grad_qv_bias = jnp.concatenate([jnp.sum(query_grad, axis=0), jnp.sum(values_grad, axis=0)])
        joined = jnp.concatenate([query_grad, key_grad, values_grad], axis=1)
        grad_qkv = scatter(grad_parts(normed, joined, me, count), count)
        normed_partial = (
            weight_product(query_grad, qkv_weight[number, 0], 1)
            + weight_product(key_grad, qkv_weight[number, 1], 1)
            + weight_product(values_grad, qkv_weight[number, 2], 1)
        )
        normed_grad = pair_sum(normed_partial, pairs)
        stream_grad, grad_ln1_gain, grad_ln1_shift = norm_backward(normed_grad, unit, scale, ln1_gain[number])
        gradient = gradient + stream_grad
        small_terms[number] = (
            grad_ln1_gain,
            grad_ln1_shift,
            grad_qv_bias,
            grad_proj_bias,
            grad_ln2_gain,
            grad_ln2_shift,
            grad_fc_bias,
            grad_out_bias,
        )
        big_terms[number] = (grad_qkv, grad_proj, grad_fc, grad_out)
    flat_small = jnp.concatenate([term for terms in small_terms for term in terms])
    flat_small = small_sum(flat_small.reshape(-1, LANES), count).reshape(-1)
    sums, start = [[] for _ in small_terms[0]], 0
    for terms in small_terms:
        for member, term in enumerate(terms):
            sums[member].append(flat_small[start:start + term.shape[0]])
            start += term.shape[0]
    (ln1_gain_sum, ln1_shift_sum, qv_bias_sum, proj_bias_sum, ln2_gain_sum, ln2_shift_sum, fc_bias_sum, out_bias_sum) = [
        jnp.stack(member) for member in sums
    ]
    qv_bias_sum = qv_bias_sum.reshape(layer_count, 2, -1)
    rows = tokens.shape[1] // count
    qkv_sum = jnp.stack([jnp.stack(jnp.split(terms[0], 3, axis=1)) for terms in big_terms])
    proj_sum = jnp.stack([terms[1].T for terms in big_terms])
    fc_sum = jnp.stack([terms[2] for terms in big_terms])
    out_sum = jnp.stack([terms[3].T for terms in big_terms])
    return (
        block_out,
        gradient,
        ln1_gain_sum,
        ln1_shift_sum,
        qkv_sum,
        qv_bias_sum,
        proj_sum,
        proj_bias_sum,
        ln2_gain_sum,
        ln2_shift_sum,
        fc_sum,
        fc_bias_sum,
        out_sum,
        out_bias_sum,
    )


def solution(mesh):
    in_specs = (
        P("dp", None),
        P("dp", None),
        P("dp", None),
        P("dp"),
        P(),
        P(),
        P(None, None, None, "tensor"),
        P(None, None, "tensor"),
        P(None, "tensor", None),
        P(),
        P(),
        P(),
        P(None, None, "tensor"),
        P(None, "tensor"),
        P(None, "tensor", None),
        P(),
    )
    out_specs = (
        P("dp", None),
        P("dp", None),
        P(),
        P(),
        P(None, None, "dp", "tensor"),
        P(None, None, "tensor"),
        P(None, "tensor", "dp"),
        P(),
        P(),
        P(),
        P(None, "dp", "tensor"),
        P(None, "tensor"),
        P(None, "tensor", "dp"),
        P(),
    )
    return jax.shard_map(
        functools.partial(on_device, mesh.shape["dp"], mesh.shape["tensor"]),
        mesh=mesh,
        in_specs=in_specs,
        out_specs=out_specs,
        check_vma=False,
    )
```

```python
import functools

import jax
import jax.numpy as jnp
from jax import lax
from jax.experimental import pallas as pl
from jax.experimental.pallas import tpu as pltpu
from jax.sharding import PartitionSpec as P

HEAD_DIM = 64
EPSILON = 1e-05
LANES = 128
HEAD_SCALE = HEAD_DIM ** (-0.5)
MASKED = -1e30
F32 = jnp.float32
BF16 = jnp.bfloat16
GELU_A = 0.7978845608028654
GELU_B = 0.044715
HIDDEN_TILE = 512
FLOWS = 3
EARLY = 0
LARGE = 24
SMALL = 16


def split_two(values):
    high = values.astype(BF16)
    return high, (values - high.astype(F32)).astype(BF16)


def product(left, right):
    return jnp.dot(left, right, preferred_element_type=F32)


def product_turned(left, right):
    return lax.dot_general(left, right, (((1,), (1,)), ((), ())), preferred_element_type=F32)


def turned_product(left, right):
    return lax.dot_general(left, right, (((0,), (0,)), ((), ())), preferred_element_type=F32)


def by_weight(pair, weight):
    return product(pair[0], weight) + product(pair[1], weight)


def by_weight_turned(pair, weight):
    return product_turned(pair[0], weight) + product_turned(pair[1], weight)


def normalize(values):
    centred = values - jnp.mean(values, axis=-1, keepdims=True)
    scale = lax.rsqrt(jnp.mean(centred * centred, axis=-1, keepdims=True) + EPSILON)
    return centred * scale, scale


def norm_backward(grad, unit, scale, norm_gain):
    gained = grad * norm_gain
    mean_grad = jnp.mean(gained, axis=-1, keepdims=True)
    mean_dot = jnp.mean(gained * unit, axis=-1, keepdims=True)
    return scale * (gained - mean_grad - unit * mean_dot)


def column_sum(values):
    return jnp.sum(values, axis=0, keepdims=True)


def gelu(values):
    bent = jnp.tanh(GELU_A * (values + GELU_B * values * values * values))
    return 0.5 * values * (1.0 + bent)


def gelu_slope(values):
    square = values * values
    bent = jnp.tanh(GELU_A * (values + GELU_B * values * square))
    inner = GELU_A * (1.0 + 3.0 * GELU_B * square)
    return 0.5 * (1.0 + bent) + 0.5 * values * (1.0 - bent * bent) * inner


def fill_mask(mask_ref, tag_column_ref, tag_row_ref):
    shape = mask_ref.shape
    same = tag_column_ref[...] == tag_row_ref[...]
    causal = lax.broadcasted_iota(jnp.int32, shape, 1) <= lax.broadcasted_iota(jnp.int32, shape, 0)
    mask_ref[...] = jnp.where(same & causal, 1.0, 0.0)


def head_pieces(values):
    high, low = split_two(values)
    return high, low


def attend_kernel(number, first, *refs):
    if first:
        x_ref, *refs = refs
        values = x_ref[...]
    else:
        m_ref, part_ref, got_ref, out_bias_ref, *refs = refs
        values = m_ref[...] + (part_ref[...] + got_ref[...]) + out_bias_ref[number - 1:number, :]
    gain_ref, shift_ref, weight_ref, bias_ref, proj_ref, tag_column_ref, tag_row_ref, *refs = refs
    if not first:
        x_out_ref, *refs = refs
        x_out_ref[...] = values
    normed_ref, qkv_ref, result_ref, logsum_ref, branch_ref, mask_ref = refs
    rows = values.shape[0]
    unit, _ = normalize(values)
    normed = unit * gain_ref[number:number + 1, :] + shift_ref[number:number + 1, :]
    normed_ref[...] = normed
    pair = split_two(normed)
    width = weight_ref.shape[-1]
    for member in range(3):
        piece = by_weight(pair, weight_ref[0, member])
        if member != 1:
            piece = piece + bias_ref[number, member // 2:member // 2 + 1, :]
        qkv_ref[:, member * width:(member + 1) * width] = piece
    fill_mask(mask_ref, tag_column_ref, tag_row_ref)
    for head in range(width // HEAD_DIM):
        low_at = head * HEAD_DIM
        query, key, value = (
            split_two(qkv_ref[:, member * width + low_at:member * width + low_at + HEAD_DIM]) for member in range(3)
        )
        queries = jnp.concatenate([query[0], query[0], query[1]], axis=1)
        keys = jnp.concatenate([key[0], key[1], key[0]], axis=1)
        both = jnp.concatenate([value[0], value[1]], axis=1)
        for start in range(0, rows, LANES):
            stop = start + LANES
            scores = product_turned(queries[start:stop], keys[:stop]) * HEAD_SCALE
            scores = jnp.where(mask_ref[start:stop, :stop] > 0.5, scores, MASKED)
            peak = jnp.max(scores, axis=1, keepdims=True)
            weights = jnp.exp(scores - peak)
            total = jnp.sum(weights, axis=1, keepdims=True)
            logsum_ref[start:stop, head:head + 1] = peak + jnp.log(total)
            high, low = split_two(weights)
            mixed = product(high, both[:stop])
            mixed = mixed[:, :HEAD_DIM] + mixed[:, HEAD_DIM:] + product(low, value[0][:stop])
            result_ref[start:stop, low_at:low_at + HEAD_DIM] = mixed / total
    branch_ref[...] = by_weight(split_two(result_ref[...]), proj_ref[0])


def mlp_kernel(
    number, x_ref, part_ref, got_ref, proj_bias_ref, gain_ref, shift_ref, fc_ref, fc_bias_ref, out_ref,
    middle_ref, normed_ref, hidden_ref, active_ref, branch_ref,
):
    values = x_ref[...] + (part_ref[...] + got_ref[...]) + proj_bias_ref[number:number + 1, :]
    middle_ref[...] = values
    unit, _ = normalize(values)
    normed = unit * gain_ref[number:number + 1, :] + shift_ref[number:number + 1, :]
    normed_ref[...] = normed
    pair = split_two(normed)
    total = None
    for start in range(0, fc_ref.shape[-1], HIDDEN_TILE):
        tile = slice(start, start + HIDDEN_TILE)
        hidden = by_weight(pair, fc_ref[0, :, tile]) + fc_bias_ref[number:number + 1, tile]
        hidden_ref[:, tile] = hidden
        active = gelu(hidden)
        active_ref[:, tile] = active
        term = by_weight(split_two(active), out_ref[0, tile, :])
        total = term if total is None else total + term
    branch_ref[...] = total


def stream_grad(number, grad_ref, x_ref, part_ref, got_ref, gain_ref, gain_sum_ref, shift_sum_ref):
    unit, scale = normalize(x_ref[...])
    arriving = part_ref[...] + got_ref[...]
    gain_sum_ref[...] = column_sum(arriving * unit)
    shift_sum_ref[...] = column_sum(arriving)
    return grad_ref[...] + norm_backward(arriving, unit, scale, gain_ref[number:number + 1, :])


def mlp_back_kernel(number, top, *refs):
    if top:
        grad_ref, *refs = refs
    else:
        above, refs = refs[:5], refs[5:]
    hidden_ref, fc_ref, out_ref, *refs = refs
    if top:
        grad = grad_ref[...]
    else:
        gain_sum_ref, shift_sum_ref, grad_ref, *refs = refs
        grad = stream_grad(number + 1, *above, gain_sum_ref, shift_sum_ref)
        grad_ref[...] = grad
    out_bias_ref, fc_bias_ref, hidden_grad_ref, branch_ref = refs
    out_bias_ref[...] = column_sum(grad)
    pair = split_two(grad)
    total = None
    for start in range(0, fc_ref.shape[-1], HIDDEN_TILE):
        tile = slice(start, start + HIDDEN_TILE)
        active_grad = by_weight_turned(pair, out_ref[0, tile, :])
        hidden_grad = gelu_slope(hidden_ref[:, tile]) * active_grad
        hidden_grad_ref[:, tile] = hidden_grad
        fc_bias_ref[:, tile] = column_sum(hidden_grad)
        term = by_weight_turned(split_two(hidden_grad), fc_ref[0, :, tile])
        total = term if total is None else total + term
    branch_ref[...] = total


def attend_back_kernel(
    number, grad_ref, middle_ref, part_ref, got_ref, gain_ref, proj_ref, weight_ref, qkv_ref, result_ref, logsum_ref,
    tag_column_ref, tag_row_ref,
    gain_sum_ref, shift_sum_ref, proj_bias_ref, bias_ref, middle_grad_ref, qkv_grad_ref, branch_ref,
    mask_ref, result_grad_ref,
):
    grad = stream_grad(number, grad_ref, middle_ref, part_ref, got_ref, gain_ref, gain_sum_ref, shift_sum_ref)
    middle_grad_ref[...] = grad
    proj_bias_ref[...] = column_sum(grad)
    result_grad_ref[...] = by_weight_turned(split_two(grad), proj_ref[0])
    fill_mask(mask_ref, tag_column_ref, tag_row_ref)
    rows, width = result_ref.shape
    for head in range(width // HEAD_DIM):
        low_at = head * HEAD_DIM
        columns = slice(low_at, low_at + HEAD_DIM)
        query, key, value = (
            split_two(qkv_ref[:, member * width + low_at:member * width + low_at + HEAD_DIM]) for member in range(3)
        )
        given = result_grad_ref[:, columns]
        given_pair = split_two(given)
        delta = jnp.sum(given * result_ref[:, columns], axis=1, keepdims=True)
        queries = jnp.concatenate([query[0], query[0], query[1]], axis=1)
        keys = jnp.concatenate([key[0], key[1], key[0]], axis=1)
        givens = jnp.concatenate([given_pair[0], given_pair[0], given_pair[1]], axis=1)
        values = jnp.concatenate([value[0], value[1], value[0]], axis=1)
        key_both = jnp.concatenate([key[0], key[1]], axis=1)
        query_both = jnp.concatenate([query[0], query[1]], axis=1)
        given_both = jnp.concatenate([given_pair[0], given_pair[1]], axis=1)
        for start in range(0, rows, LANES):
            stop = start + LANES
            scores = product_turned(queries[start:stop], keys[:stop]) * HEAD_SCALE
            scores = jnp.where(mask_ref[start:stop, :stop] > 0.5, scores, MASKED)
            weights = jnp.exp(scores - logsum_ref[start:stop, head:head + 1])
            weights_grad = product_turned(givens[start:stop], values[:stop])
            scores_grad = weights * (weights_grad - delta[start:stop]) * HEAD_SCALE
            high, low = split_two(scores_grad)
            mixed = product(high, key_both[:stop])
            qkv_grad_ref[start:stop, columns] = (
                mixed[:, :HEAD_DIM] + mixed[:, HEAD_DIM:] + product(low, key[0][:stop])
            )
            mixed = turned_product(high, query_both[start:stop])
            key_grad = mixed[:, :HEAD_DIM] + mixed[:, HEAD_DIM:] + turned_product(low, query[0][start:stop])
            high, low = split_two(weights)
            mixed = turned_product(high, given_both[start:stop])
            value_grad = mixed[:, :HEAD_DIM] + mixed[:, HEAD_DIM:] + turned_product(low, given_pair[0][start:stop])
            for member, term in ((1, key_grad), (2, value_grad)):
                at = slice(member * width + low_at, member * width + low_at + HEAD_DIM)
                if start == 0:
                    qkv_grad_ref[:stop, at] = term
                else:
                    qkv_grad_ref[:start, at] += term[:start]
                    qkv_grad_ref[start:stop, at] = term[start:]
    total = None
    for member in range(3):
        piece = qkv_grad_ref[:, member * width:(member + 1) * width]
        if member != 1:
            bias_ref[:, (member // 2) * width:(member // 2 + 1) * width] = column_sum(piece)
        term = by_weight_turned(split_two(piece), weight_ref[0, member])
        total = term if total is None else total + term
    branch_ref[...] = total


def input_grad_kernel(grad_ref, x_ref, part_ref, got_ref, gain_ref, gain_sum_ref, shift_sum_ref, out_ref):
    out_ref[...] = stream_grad(0, grad_ref, x_ref, part_ref, got_ref, gain_ref, gain_sum_ref, shift_sum_ref)


def block_out_kernel(number, middle_ref, part_ref, got_ref, out_bias_ref, live_ref, out_ref):
    values = middle_ref[...] + (part_ref[...] + got_ref[...]) + out_bias_ref[number:number + 1, :]
    out_ref[...] = values * live_ref[...]


def whole():
    return pl.BlockSpec(memory_space=pltpu.VMEM)


class Fetched:
    def __init__(self, source, target, semaphore):
        self.copy = pltpu.make_async_copy(source, target, semaphore)
        self.copy.start()
        self.target = target
        self.shape = target.shape
        self.waiting = True

    def __getitem__(self, index):
        if self.waiting:
            self.copy.wait()
            self.waiting = False
        return self.target[index]


class Halves:
    def __init__(self, upper, lower):
        self.refs = upper, lower

    def __getitem__(self, index):
        return jnp.concatenate([ref[...] for ref in self.refs], axis=0)

    def __setitem__(self, index, values):
        rows = values.shape[0] // 2
        self.refs[0][...], self.refs[1][...] = values[:rows], values[rows:]


def wrapped(kernel, operand_kinds, out_kinds, layers, *refs):
    refs = list(refs)
    semaphores = refs[len(refs) - len(layers):]
    targets = refs[len(refs) - 2 * len(layers):len(refs) - len(layers)]
    refs = refs[:len(refs) - 2 * len(layers)]
    made, fetched = [], 0
    for kind in operand_kinds + out_kinds:
        if kind == "halves":
            made.append(Halves(refs.pop(0), refs.pop(0)))
        elif kind == "layer":
            source = refs.pop(0).at[pl.ds(layers[fetched], 1)]
            made.append(Fetched(source, targets[fetched], semaphores[fetched]))
            fetched += 1
        else:
            made.append(refs.pop(0))
    kernel(*made, *refs)


def run(kernel, operands, outs, flops, scratch=(), limit=LARGE):
    specs, arrays, layers, kinds, moved = [], [], [], [], 0
    scratch, semaphores = list(scratch), []
    for operand in operands:
        if isinstance(operand, tuple):
            array, number = operand
            kinds.append("layer")
            layers.append(number)
            specs.append(pl.BlockSpec(memory_space=pltpu.MemorySpace.HBM))
            scratch.append(pltpu.VMEM((1,) + array.shape[1:], array.dtype))
            semaphores.append(pltpu.SemaphoreType.DMA(()))
            arrays.append(pltpu.with_memory_space_constraint(array, pltpu.MemorySpace.HBM))
        elif isinstance(operand, list):
            kinds.append("halves")
            specs += [whole()] * 2
            arrays += operand
        else:
            kinds.append("whole")
            specs.append(whole())
            arrays.append(operand)
    shapes, out_kinds = [], []
    for out in outs:
        if isinstance(out, list):
            out_kinds.append("halves")
            shapes += [jax.ShapeDtypeStruct((out[0][0] // 2, out[0][1]), F32)] * 2
        else:
            out_kinds.append("whole")
            shapes.append(jax.ShapeDtypeStruct(out, F32))
    moved = sum(4 * shape.size for shape in shapes)
    results = list(
        pl.pallas_call(
            functools.partial(wrapped, kernel, kinds, out_kinds, layers),
            out_shape=shapes,
            in_specs=specs,
            out_specs=[whole()] * len(shapes),
            scratch_shapes=scratch + semaphores,
            compiler_params=pltpu.CompilerParams(vmem_limit_bytes=limit * 2**20),
            cost_estimate=pl.CostEstimate(flops=flops, bytes_accessed=moved, transcendentals=0),
        )(*arrays)
    )
    return [[results.pop(0), results.pop(0)] if kind == "halves" else results.pop(0) for kind in out_kinds]


def bit_orders(count):
    bits = [1 << at for at in range(count.bit_length() - 1)]
    lead, rest = bits[:FLOWS], bits[FLOWS:]
    return [lead[at:] + lead[:at] for at in range(FLOWS)], rest


def block_masks(order):
    masks = [0]
    for bit in reversed(order):
        masks = masks + [mask + bit for mask in masks]
    return masks


def grad_kernel(mask_lists, permuted, pairs, me_ref, *refs):
    ins, refs = refs[: 2 * pairs], refs[2 * pairs:]
    outs, (turned_high, turned_low, high_ref, low_ref) = refs[: 2 * FLOWS], refs[2 * FLOWS:]
    depth = high_ref.shape[0]
    half = depth // 2
    start = 0
    for at in range(pairs):
        a_ref, b_ref = ins[2 * at], ins[2 * at + 1]
        width = b_ref.shape[1] // FLOWS
        if not permuted:
            turned_high[...], turned_low[...] = split_two(a_ref[...].T)
        for flow, masks in enumerate(mask_lists):
            if permuted:
                high_ref[...], low_ref[...] = split_two(a_ref[flow])
            else:
                rows = depth // len(masks)
                for place, mask in enumerate(masks):
                    source = pl.ds(pl.multiple_of((me_ref[0] ^ mask) * rows, 16), rows)
                    target = pl.ds(place * rows, rows)
                    high_ref[target, :] = turned_high[source, :]
                    low_ref[target, :] = turned_low[source, :]
            part_high, part_low = split_two(b_ref[:, flow * width:(flow + 1) * width])
            for which in (1, 0):
                rows_at = pl.ds(which * half, half)
                outs[2 * flow + 1 - which][:, start:start + width] = (
                    product(high_ref[rows_at, :], part_high)
                    + product(high_ref[rows_at, :], part_low)
                    + product(low_ref[rows_at, :], part_high)
                )
        start += width


def grad_parts(pairs, names, me, count):
    orders, rest = bit_orders(count)
    mask_lists = [block_masks(order + rest) for order in orders]
    tokens, depth = pairs[0][0].shape
    rows = depth // count
    permuted = rows % 16 != 0
    operands, columns = [], 0
    for left, right in pairs:
        if permuted:
            blocks = left.T.reshape(count, rows, tokens)
            left = jnp.stack(
                [jnp.take(blocks, me ^ jnp.array(masks, jnp.int32), axis=0).reshape(depth, tokens) for masks in mask_lists]
            )
        operands += [left, right]
        columns += right.shape[1]
    shapes = [jax.ShapeDtypeStruct((depth // 2, columns // FLOWS), F32)] * (2 * FLOWS)
    outs = pl.pallas_call(
        functools.partial(grad_kernel, mask_lists, permuted, len(pairs)),
        out_shape=shapes,
        in_specs=[pl.BlockSpec(memory_space=pltpu.SMEM)] + [whole()] * len(operands),
        out_specs=[whole()] * len(shapes),
        scratch_shapes=[pltpu.VMEM((depth, tokens), BF16)] * 4,
        compiler_params=pltpu.CompilerParams(vmem_limit_bytes=LARGE * 2**20),
        cost_estimate=pl.CostEstimate(flops=10**6, bytes_accessed=10**5, transcendentals=0),
    )(me.reshape(1), *operands)
    parts = [(name, right.shape[1] // FLOWS) for name, (_, right) in zip(names, pairs)]
    return {"send": list(outs[0::2]), "keep": list(outs[1::2]), "phase": 0, "parts": parts}


def fold_kernel(pieces, members, *refs):
    gots, keeps, outs = refs[: FLOWS * members], refs[FLOWS * members : 2 * FLOWS * members], refs[2 * FLOWS * members :]
    half = gots[0].shape[0] // 2
    for number, piece in enumerate(pieces):
        at = 0
        for flow in piece:
            for member in range(members):
                got, keep = gots[FLOWS * member + flow], keeps[FLOWS * member + flow]
                columns = slice(at, at + got.shape[1])
                at += got.shape[1]
                for which in (1, 0):
                    rows = slice(which * half, (which + 1) * half)
                    outs[len(pieces) * (1 - which) + number][:, columns] = got[rows, :] + keep[rows, :]


class Scatter:
    def __init__(self, count):
        self.count = count
        self.orders, self.rest = bit_orders(count)
        self.axes = [order[0] for order in self.orders]
        self.before, self.last = [], []
        self.flat, self.done = None, 0

    def swap(self, values, bit):
        return lax.ppermute(values, "dp", [(one, one ^ bit) for one in range(self.count)])

    def launch(self, chunk, tokens=(), ride=None, step=False):
        gots, arrived = [None] * FLOWS, []
        for axis, bit in enumerate(self.axes):
            flow = [order[chunk["phase"]] for order in self.orders].index(bit)
            waits = list(tokens) + self.before
            if axis >= EARLY and self.last:
                waits.append(self.last[axis - EARLY])
            (send,) = after([chunk["send"][flow]], waits)
            gots[flow] = self.swap(send, bit)
            arrived.append(gots[flow])
        chunk["got"] = gots
        if ride:
            arrived.append(self.ride(*ride))
        if step:
            arrived.append(self.step())
        self.before, self.last = self.last, arrived

    def step(self):
        (send,) = after([self.flat], self.last)
        got = self.swap(send, 1 << self.done)
        self.flat, self.done = self.flat + got, self.done + 1
        return got

    def ride(self, chunk, piece):
        (send,), keep = after([chunk["send"][piece]], self.last), chunk["keep"][piece]
        for bit in self.rest[:-1]:
            total = keep + self.swap(send, bit)
            half = total.shape[0] // 2
            keep, send = total[:half], total[half:]
        got = self.swap(send, self.rest[-1])
        chunk["keep"][piece], chunk["got"][piece] = keep, got
        return got

    def fold(self, *chunks, pieces=tuple((flow,) for flow in range(FLOWS))):
        rows = chunks[0]["got"][0].shape[0]
        width = sum(chunk["got"][0].shape[1] for chunk in chunks)
        outs = [(rows // 2, len(piece) * width) for piece in pieces] * 2
        operands = [got for chunk in chunks for got in chunk["got"]] + [keep for chunk in chunks for keep in chunk["keep"]]
        result = run(functools.partial(fold_kernel, pieces, len(chunks)), operands, outs, FLOWS * rows * width, limit=SMALL)
        return {
            "parts": [part for chunk in chunks for part in chunk["parts"]],
            "phase": chunks[0]["phase"] + 1,
            "pieces": pieces,
            "send": result[:len(pieces)],
            "keep": result[len(pieces):],
            "got": [None] * len(pieces),
        }


def pack_kernel(*refs):
    *terms, out_ref = refs
    at = 0
    for term in terms:
        size = term.shape[1]
        out_ref[:, at:at + size] = term[...]
        at += size


def finish_kernel(layout, small, *refs):
    pairs = sum(len(pieces) for _, pieces in layout)
    keeps, gots, small_ref = refs[:pairs], refs[pairs:2 * pairs], refs[2 * pairs]
    out_ref, fc_ref, proj_ref, qkv_ref, *small_refs = refs[2 * pairs + 1:]
    number = 0
    for parts, pieces in layout:
        width = sum(size for _, size in parts)
        for piece in pieces:
            total = keeps[number][...] + gots[number][...]
            number += 1
            for place, flow in enumerate(piece):
                at = place * width
                for (name, layer), size in parts:
                    block = total[:, at:at + size]
                    at += size
                    if name == "qkv":
                        qkv_ref[layer, flow] = block
                    else:
                        ref = {"out": out_ref, "fc": fc_ref, "proj": proj_ref}[name]
                        ref[layer, :, flow * size:(flow + 1) * size] = block
    at = 0
    for ref, (layers, size) in zip(small_refs, small):
        for layer in range(layers):
            ref[layer:layer + 1, :] = small_ref[:, at:at + size]
            at += size


def after(values, tokens):
    if not tokens:
        return values
    return lax.optimization_barrier((values, list(tokens)))[0]


def on_device(
    count,
    pair,
    tokens,
    cotangent,
    doc_ids,
    live_rows,
    ln1_gain,
    ln1_shift,
    qkv_weight,
    qv_bias,
    proj_weight,
    proj_bias,
    ln2_gain,
    ln2_shift,
    fc_weight,
    fc_bias,
    out_weight,
    out_bias,
):
    row_count, depth = tokens.shape
    width, hidden = qkv_weight.shape[-1], fc_weight.shape[-1]
    top = qkv_weight.shape[0] - 1
    me = lax.axis_index("dp").astype(jnp.int32)
    position = jnp.arange(row_count, dtype=jnp.int32)
    living = position < live_rows[0]
    doc_tags = jnp.where(living, doc_ids[0], -1)
    tags = [doc_tags[:, None], doc_tags[None, :]]
    live = living[:, None].astype(F32)
    model, half, wide, line = (row_count, depth), (row_count, width), (row_count, hidden), (1, depth)
    mask_scratch = pltpu.VMEM((row_count, row_count), F32)
    macs = row_count * depth * hidden

    def exchange(halves):
        return [lax.ppermute(part, "tensor", [(one, one ^ 1) for one in range(pair)]) for part in halves]

    stored = []
    entering = [tokens]
    for number in range(top + 1):
        first = number == 0
        outs = [] if first else [model]
        outs += [model, (row_count, 3 * width), half, (row_count, LANES), [model]]
        result = run(
            functools.partial(attend_kernel, number, first),
            entering + ([] if first else [out_bias])
            + [ln1_gain, ln1_shift, (qkv_weight, number), qv_bias, (proj_weight, number)] + tags,
            outs, 8 * macs, [mask_scratch],
        )
        stream = tokens if first else result[0]
        normed, qkv, mixed, logsum, branch = result[-5:]
        middle, normed_two, hidden_in, active, branch_two = run(
            functools.partial(mlp_kernel, number),
            [stream, branch, exchange(branch), proj_bias, ln2_gain, ln2_shift, (fc_weight, number), fc_bias, (out_weight, number)],
            [model, model, wide, wide, [model]], 8 * macs,
        )
        entering = [middle, branch_two, exchange(branch_two)]
        stored.append((stream, normed, qkv, mixed, logsum, middle, normed_two, hidden_in, active))

    scatter = Scatter(count)
    small = {}

    def mlp_back(number, operands):
        is_top = number == top
        hidden_in = stored[number][7]
        outs = [] if is_top else [line, line, model]
        result = run(
            functools.partial(mlp_back_kernel, number, is_top),
            operands + [hidden_in, (fc_weight, number), (out_weight, number)],
            outs + [line, (1, hidden), wide, [model]], 24 * macs,
        )
        if is_top:
            grad = operands[0]
        else:
            small["ln1_gain", number + 1], small["ln1_shift", number + 1], grad = result[:3]
        small["out_bias", number], small["fc_bias", number], hidden_grad, branch = result[-4:]
        return grad, hidden_grad, branch

    def attend_back(number, grad, branch, got):
        stream, normed, qkv, mixed, logsum, middle = stored[number][:6]
        result = run(
            functools.partial(attend_back_kernel, number),
            [grad, middle, branch, got, ln2_gain, (proj_weight, number), (qkv_weight, number), qkv, mixed, logsum] + tags,
            [line, line, line, (1, 2 * width), model, (row_count, 3 * width), [model]], 32 * macs,
            [mask_scratch, pltpu.VMEM(half, F32)],
        )
        (small["ln2_gain", number], small["ln2_shift", number], small["proj_bias", number], small["qv_bias", number]) = result[:4]
        return result[4:]

    def out_parts(number, grad):
        return grad_parts([(grad, stored[number][8])], [("out", number)], me, count)

    def fc_parts(number, hidden_grad):
        return grad_parts([(stored[number][6], hidden_grad)], [("fc", number)], me, count)

    def mix_parts(number, middle_grad, qkv_grad):
        return grad_parts(
            [(middle_grad, stored[number][3]), (stored[number][1], qkv_grad)], [("proj", number), ("qkv", number)], me, count
        )

    grad = cotangent * live
    above, first_chunks = [grad], None
    for number in reversed(range(top + 1)):
        if number == top:
            out_chunk = out_parts(number, grad)
            scatter.launch(out_chunk)
            grad, hidden_grad, branch = mlp_back(number, after(above, out_chunk["keep"][:1]))
            got = exchange(branch)
            fc_chunk = fc_parts(number, hidden_grad)
            scatter.launch(fc_chunk)
        else:
            grad, hidden_grad, branch = mlp_back(number, after(above, scatter.before))
            got = exchange(branch)
            out_chunk = out_parts(number, grad)
            scatter.launch(out_chunk, branch)
        got = after(got, scatter.before)
        middle_grad, qkv_grad, branch = attend_back(number, grad, branch, got)
        got = exchange(branch)
        if number == top:
            mix_chunk = mix_parts(number, middle_grad, qkv_grad)
            scatter.launch(mix_chunk)
            first_chunks = out_chunk, fc_chunk, mix_chunk
        else:
            first = scatter.fold(*first_chunks[:2])
            scatter.launch(first, branch)
            fc_chunk = fc_parts(number, hidden_grad)
            scatter.launch(fc_chunk)
            mix_chunk = mix_parts(number, middle_grad, qkv_grad)
        above = [middle_grad, stored[number][0], branch, got, ln1_gain]
    gain_sum, shift_sum, input_grad = run(input_grad_kernel, above, [line, line, model], row_count * depth * 16)
    small["ln1_gain", 0], small["ln1_shift", 0] = gain_sum, shift_sum
    block_out = run(
        functools.partial(block_out_kernel, top), entering + [out_bias, live], [model], row_count * depth * 4
    )[0]
    names = ("ln1_gain", "ln1_shift", "qv_bias", "proj_bias", "ln2_gain", "ln2_shift", "fc_bias", "out_bias")
    terms = [small[name, number] for name in names for number in range(top + 1)]
    flat = run(pack_kernel, terms, [(1, sum(term.shape[1] for term in terms))], 1000, limit=SMALL)[0]
    scatter.flat = flat

    two, one = ((0, 1), (2,)), ((0, 1, 2),)
    first = scatter.fold(first)
    scatter.launch(first)
    second = scatter.fold(first_chunks[2], out_chunk)
    first = scatter.fold(first, pieces=two)
    scatter.launch(second, [flat], ride=(first, 0), step=True)
    third = scatter.fold(fc_chunk)
    scatter.launch(third, [block_out], ride=(first, 1), step=True)
    second = scatter.fold(second)
    scatter.launch(second)
    fourth = mix_chunk
    second = scatter.fold(second, pieces=two)
    scatter.launch(fourth, ride=(second, 0), step=True)
    third = scatter.fold(third)
    scatter.launch(third, step=True)
    fourth = scatter.fold(fourth)
    scatter.launch(fourth, ride=(second, 1))
    fourth, third = scatter.fold(fourth), scatter.fold(third, pieces=one)
    scatter.launch(fourth, ride=(third, 0))
    fourth = scatter.fold(fourth, pieces=one)
    scatter.ride(fourth, 0)
    while 1 << scatter.done < count:
        scatter.step()
    chunks = (first, second, third, fourth)

    layers = top + 1
    rows = depth // count
    sizes = [(layers, small[name, 0].shape[1]) for name in names]
    result = run(
        functools.partial(finish_kernel, [(chunk["parts"], chunk["pieces"]) for chunk in chunks], sizes),
        [keep for chunk in chunks for keep in chunk["keep"]] + [got for chunk in chunks for got in chunk["got"]] + [scatter.flat],
        [(layers, rows, hidden), (layers, rows, hidden), (layers, rows, width), (layers, 3, rows, width)] + sizes,
        1000,
    )
    out_sum, fc_sum, proj_sum, qkv_sum, *sums = result
    ln1_gain_sum, ln1_shift_sum, qv_bias_sum, proj_bias_sum, ln2_gain_sum, ln2_shift_sum, fc_bias_sum, out_bias_sum = sums
    return (
        block_out,
        input_grad,
        ln1_gain_sum,
        ln1_shift_sum,
        qkv_sum,
        qv_bias_sum.reshape(layers, 2, width),
        proj_sum.transpose(0, 2, 1),
        proj_bias_sum,
        ln2_gain_sum,
        ln2_shift_sum,
        fc_sum,
        fc_bias_sum,
        out_sum.transpose(0, 2, 1),
        out_bias_sum,
    )


def solution(mesh):
    in_specs = (
        P("dp", None),
        P("dp", None),
        P("dp", None),
        P("dp"),
        P(),
        P(),
        P(None, None, None, "tensor"),
        P(None, None, "tensor"),
        P(None, "tensor", None),
        P(),
        P(),
        P(),
        P(None, None, "tensor"),
        P(None, "tensor"),
        P(None, "tensor", None),
        P(),
    )
    out_specs = (
        P("dp", None),
        P("dp", None),
        P(),
        P(),
        P(None, None, "dp", "tensor"),
        P(None, None, "tensor"),
        P(None, "tensor", "dp"),
        P(),
        P(),
        P(),
        P(None, "dp", "tensor"),
        P(None, "tensor"),
        P(None, "tensor", "dp"),
        P(),
    )
    return jax.shard_map(
        functools.partial(on_device, mesh.shape["dp"], mesh.shape["tensor"]),
        mesh=mesh,
        in_specs=in_specs,
        out_specs=out_specs,
        check_vma=False,
    )
```

```python
import functools

import jax
import jax.numpy as jnp
from jax import lax
from jax.experimental import pallas as pl
from jax.experimental.pallas import tpu as pltpu
from jax.sharding import PartitionSpec as P

HEAD_DIM = 64
EPSILON = 1e-05
LANES = 128
HEAD_SCALE = HEAD_DIM ** (-0.5)
MASKED = -1e30
F32 = jnp.float32
BF16 = jnp.bfloat16
GELU_A = 0.7978845608028654
GELU_B = 0.044715
HIDDEN_TILE = 512
FLOWS = 3
LARGE = 24
LAST_SHARES = (4, 3, 2)
SMALL = 16
ROW_BLOCK = 384


def split_two(values):
    high = values.astype(BF16)
    return high, (values - high.astype(F32)).astype(BF16)


def product(left, right):
    return jnp.dot(left, right, preferred_element_type=F32)


def product_turned(left, right):
    return lax.dot_general(left, right, (((1,), (1,)), ((), ())), preferred_element_type=F32)


def turned_product(left, right):
    return lax.dot_general(left, right, (((0,), (0,)), ((), ())), preferred_element_type=F32)


def by_weight(pair, weight):
    return product(pair[0], weight) + product(pair[1], weight)


def by_weight_turned(pair, weight):
    return product_turned(pair[0], weight) + product_turned(pair[1], weight)


def normalize(values):
    centred = values - jnp.mean(values, axis=-1, keepdims=True)
    scale = lax.rsqrt(jnp.mean(centred * centred, axis=-1, keepdims=True) + EPSILON)
    return centred * scale, scale


def norm_backward(grad, unit, scale, norm_gain):
    gained = grad * norm_gain
    mean_grad = jnp.mean(gained, axis=-1, keepdims=True)
    mean_dot = jnp.mean(gained * unit, axis=-1, keepdims=True)
    return scale * (gained - mean_grad - unit * mean_dot)


def column_sum(values):
    return jnp.sum(values, axis=0, keepdims=True)


def gelu(values):
    bent = jnp.tanh(GELU_A * (values + GELU_B * values * values * values))
    return 0.5 * values * (1.0 + bent)


def gelu_slope(values):
    square = values * values
    bent = jnp.tanh(GELU_A * (values + GELU_B * values * square))
    inner = GELU_A * (1.0 + 3.0 * GELU_B * square)
    return 0.5 * (1.0 + bent) + 0.5 * values * (1.0 - bent * bent) * inner


def fill_mask(mask_ref, doc_ref, live_ref):
    shape = mask_ref.shape
    position = lax.broadcasted_iota(jnp.int32, (8, shape[1]), 1)
    documents = jnp.broadcast_to(doc_ref[...], (8, shape[1]))
    tags = jnp.where(position < live_ref[0], documents, -1).astype(F32)
    same = tags.T[:, :1] == tags[:1, :]
    causal = lax.broadcasted_iota(jnp.int32, shape, 1) <= lax.broadcasted_iota(jnp.int32, shape, 0)
    mask_ref[...] = jnp.where(same & causal, 1.0, 0.0)


def living(shape, live_ref):
    return jnp.where(lax.broadcasted_iota(jnp.int32, shape, 0) < live_ref[0], 1.0, 0.0)


def attend_kernel(number, first, *refs):
    if first:
        x_ref, *refs = refs
        values = x_ref[...]
    else:
        m_ref, part_ref, got_ref, out_bias_ref, *refs = refs
        values = m_ref[...] + (part_ref[...] + got_ref[...]) + out_bias_ref[number - 1:number, :]
    gain_ref, shift_ref, weight_ref, bias_ref, proj_ref, doc_ref, live_ref, *refs = refs
    if not first:
        x_out_ref, *refs = refs
        x_out_ref[...] = values
    normed_ref, qkv_ref, result_ref, logsum_ref, branch_ref, mask_ref = refs
    rows = values.shape[0]
    unit, _ = normalize(values)
    normed = unit * gain_ref[number:number + 1, :] + shift_ref[number:number + 1, :]
    normed_ref[...] = normed
    pair = split_two(normed)
    width = weight_ref.shape[-1]
    for member in range(3):
        piece = by_weight(pair, weight_ref[0, member])
        if member != 1:
            piece = piece + bias_ref[number, member // 2:member // 2 + 1, :]
        qkv_ref[:, member * width:(member + 1) * width] = piece
    fill_mask(mask_ref, doc_ref, live_ref)
    for head in range(width // HEAD_DIM):
        low_at = head * HEAD_DIM
        query, key, value = (
            split_two(qkv_ref[:, member * width + low_at:member * width + low_at + HEAD_DIM]) for member in range(3)
        )
        queries = jnp.concatenate([query[0], query[0], query[1]], axis=1)
        keys = jnp.concatenate([key[0], key[1], key[0]], axis=1)
        both = jnp.concatenate([value[0], value[1]], axis=1)
        for start in range(0, rows, ROW_BLOCK):
            stop = start + ROW_BLOCK
            scores = product_turned(queries[start:stop], keys[:stop]) * HEAD_SCALE
            scores = jnp.where(mask_ref[start:stop, :stop] > 0.5, scores, MASKED)
            peak = jnp.max(scores, axis=1, keepdims=True)
            weights = jnp.exp(scores - peak)
            total = jnp.sum(weights, axis=1, keepdims=True)
            logsum_ref[start:stop, head:head + 1] = peak + jnp.log(total)
            high, low = split_two(weights)
            mixed = product(high, both[:stop])
            mixed = mixed[:, :HEAD_DIM] + mixed[:, HEAD_DIM:] + product(low, value[0][:stop])
            result_ref[start:stop, low_at:low_at + HEAD_DIM] = mixed / total
    branch_ref[...] = by_weight(split_two(result_ref[...]), proj_ref[0])


def mlp_kernel(
    number, x_ref, part_ref, got_ref, proj_bias_ref, gain_ref, shift_ref, fc_ref, fc_bias_ref, out_ref,
    middle_ref, normed_ref, hidden_ref, active_ref, branch_ref,
):
    values = x_ref[...] + (part_ref[...] + got_ref[...]) + proj_bias_ref[number:number + 1, :]
    middle_ref[...] = values
    unit, _ = normalize(values)
    normed = unit * gain_ref[number:number + 1, :] + shift_ref[number:number + 1, :]
    normed_ref[...] = normed
    pair = split_two(normed)
    tiles = [slice(start, start + HIDDEN_TILE) for start in range(0, fc_ref.shape[-1], HIDDEN_TILE)]
    entered = lambda tile: by_weight(pair, fc_ref[0, :, tile]) + fc_bias_ref[number:number + 1, tile]
    total, hidden = None, entered(tiles[0])
    for at, tile in enumerate(tiles):
        later = entered(tiles[at + 1]) if at + 1 < len(tiles) else None
        active = gelu(hidden)
        term = by_weight(split_two(active), out_ref[0, tile, :])
        total = term if total is None else total + term
        hidden_ref[:, tile], active_ref[:, tile] = hidden, active
        hidden = later
    branch_ref[...] = total


def stream_grad(number, grad_ref, x_ref, part_ref, got_ref, gain_ref, gain_sum_ref, shift_sum_ref):
    unit, scale = normalize(x_ref[...])
    arriving = part_ref[...] + got_ref[...]
    gain_sum_ref[...] = column_sum(arriving * unit)
    shift_sum_ref[...] = column_sum(arriving)
    return grad_ref[...] + norm_backward(arriving, unit, scale, gain_ref[number:number + 1, :])


def mlp_back_kernel(number, top, *refs):
    if top:
        cotangent_ref, live_ref, *refs = refs
    else:
        above, refs = refs[:5], refs[5:]
    hidden_ref, fc_ref, out_ref, *refs = refs
    if top:
        grad = Masked(cotangent_ref, live_ref)[...]
    else:
        gain_sum_ref, shift_sum_ref, grad_ref, *refs = refs
        grad = stream_grad(number + 1, *above, gain_sum_ref, shift_sum_ref)
        grad_ref[...] = grad
    out_bias_ref, fc_bias_ref, hidden_grad_ref, branch_ref = refs
    out_bias_ref[...] = column_sum(grad)
    pair = split_two(grad)
    tiles = [slice(start, start + HIDDEN_TILE) for start in range(0, fc_ref.shape[-1], HIDDEN_TILE)]
    total, active_grad = None, by_weight_turned(pair, out_ref[0, tiles[0], :])
    for at, tile in enumerate(tiles):
        later = by_weight_turned(pair, out_ref[0, tiles[at + 1], :]) if at + 1 < len(tiles) else None
        hidden_grad = gelu_slope(hidden_ref[:, tile]) * active_grad
        active_grad = later
        hidden_grad_ref[:, tile] = hidden_grad
        fc_bias_ref[:, tile] = column_sum(hidden_grad)
        term = by_weight_turned(split_two(hidden_grad), fc_ref[0, :, tile])
        total = term if total is None else total + term
    branch_ref[...] = total


def attend_back_kernel(
    number, top, grad_ref, middle_ref, part_ref, got_ref, gain_ref, proj_ref, weight_ref, qkv_ref, result_ref, logsum_ref,
    doc_ref, live_ref,
    gain_sum_ref, shift_sum_ref, proj_bias_ref, bias_ref, middle_grad_ref, qkv_grad_ref, branch_ref,
    mask_ref, result_grad_ref,
):
    if top:
        grad_ref = Masked(grad_ref, live_ref)
    grad = stream_grad(number, grad_ref, middle_ref, part_ref, got_ref, gain_ref, gain_sum_ref, shift_sum_ref)
    middle_grad_ref[...] = grad
    proj_bias_ref[...] = column_sum(grad)
    result_grad_ref[...] = by_weight_turned(split_two(grad), proj_ref[0])
    fill_mask(mask_ref, doc_ref, live_ref)
    rows, width = result_ref.shape
    for head in range(width // HEAD_DIM):
        low_at = head * HEAD_DIM
        columns = slice(low_at, low_at + HEAD_DIM)
        query, key, value = (
            split_two(qkv_ref[:, member * width + low_at:member * width + low_at + HEAD_DIM]) for member in range(3)
        )
        given = result_grad_ref[:, columns]
        given_pair = split_two(given)
        delta = jnp.sum(given * result_ref[:, columns], axis=1, keepdims=True)
        queries = jnp.concatenate([query[0], query[0], query[1]], axis=1)
        keys = jnp.concatenate([key[0], key[1], key[0]], axis=1)
        givens = jnp.concatenate([given_pair[0], given_pair[0], given_pair[1]], axis=1)
        values = jnp.concatenate([value[0], value[1], value[0]], axis=1)
        key_both = jnp.concatenate([key[0], key[1]], axis=1)
        query_both = jnp.concatenate([query[0], query[1]], axis=1)
        given_both = jnp.concatenate([given_pair[0], given_pair[1]], axis=1)
        for start in range(0, rows, ROW_BLOCK):
            stop = start + ROW_BLOCK
            scores = product_turned(queries[start:stop], keys[:stop]) * HEAD_SCALE
            scores = jnp.where(mask_ref[start:stop, :stop] > 0.5, scores, MASKED)
            weights = jnp.exp(scores - logsum_ref[start:stop, head:head + 1])
            weights_grad = product_turned(givens[start:stop], values[:stop])
            scores_grad = weights * (weights_grad - delta[start:stop]) * HEAD_SCALE
            high, low = split_two(scores_grad)
            mixed = product(high, key_both[:stop])
            qkv_grad_ref[start:stop, columns] = (
                mixed[:, :HEAD_DIM] + mixed[:, HEAD_DIM:] + product(low, key[0][:stop])
            )
            mixed = turned_product(high, query_both[start:stop])
            key_grad = mixed[:, :HEAD_DIM] + mixed[:, HEAD_DIM:] + turned_product(low, query[0][start:stop])
            high, low = split_two(weights)
            mixed = turned_product(high, given_both[start:stop])
            value_grad = mixed[:, :HEAD_DIM] + mixed[:, HEAD_DIM:] + turned_product(low, given_pair[0][start:stop])
            for member, term in ((1, key_grad), (2, value_grad)):
                at = slice(member * width + low_at, member * width + low_at + HEAD_DIM)
                if start == 0:
                    qkv_grad_ref[:stop, at] = term
                else:
                    qkv_grad_ref[:start, at] += term[:start]
                    qkv_grad_ref[start:stop, at] = term[start:]
    total = None
    for member in range(3):
        piece = qkv_grad_ref[:, member * width:(member + 1) * width]
        if member != 1:
            bias_ref[:, (member // 2) * width:(member // 2 + 1) * width] = column_sum(piece)
        term = by_weight_turned(split_two(piece), weight_ref[0, member])
        total = term if total is None else total + term
    branch_ref[...] = total


def input_grad_kernel(grad_ref, x_ref, part_ref, got_ref, gain_ref, gain_sum_ref, shift_sum_ref, out_ref):
    out_ref[...] = stream_grad(0, grad_ref, x_ref, part_ref, got_ref, gain_ref, gain_sum_ref, shift_sum_ref)


def block_out_kernel(number, middle_ref, part_ref, got_ref, out_bias_ref, live_ref, out_ref):
    values = middle_ref[...] + (part_ref[...] + got_ref[...]) + out_bias_ref[number:number + 1, :]
    out_ref[...] = values * living(values.shape, live_ref)


def whole():
    return pl.BlockSpec(memory_space=pltpu.VMEM)


class Fetched:
    def __init__(self, source, target, semaphore):
        self.copy = pltpu.make_async_copy(source, target, semaphore)
        self.copy.start()
        self.target = target
        self.shape = target.shape
        self.waiting = True

    def __getitem__(self, index):
        if self.waiting:
            self.copy.wait()
            self.waiting = False
        return self.target[index]


class Masked:
    def __init__(self, ref, live_ref):
        self.ref, self.live_ref, self.shape = ref, live_ref, ref.shape

    def __getitem__(self, index):
        return self.ref[index] * living(self.shape, self.live_ref)


class Saved:
    def __init__(self, target, stage, semaphores, late):
        self.target, self.stage, self.semaphores, self.late = target, stage, semaphores, late
        self.shape, self.copies = stage.shape, []

    def push(self, index):
        source, target = self.stage.at[index], self.target.at[index]
        self.copies.append(pltpu.make_async_copy(source, target, self.semaphores.at[len(self.copies)]))
        self.copies[-1].start()

    def __getitem__(self, index):
        return self.stage[index]

    def __setitem__(self, index, values):
        self.stage[index] = values
        if not self.late:
            self.push(index)

    def finish(self):
        if self.late:
            self.push(Ellipsis)
        for copy in self.copies:
            copy.wait()


class Halves:
    def __init__(self, upper, lower):
        self.refs = upper, lower

    def __getitem__(self, index):
        return jnp.concatenate([ref[...] for ref in self.refs], axis=0)

    def __setitem__(self, index, values):
        rows = values.shape[0] // 2
        self.refs[0][...], self.refs[1][...] = values[:rows], values[rows:]


def wrapped(kernel, operand_kinds, out_kinds, owned, *refs):
    refs = list(refs)
    mine, refs = refs[len(refs) - owned:], refs[:len(refs) - owned]
    made, saved = [], []
    for kind, detail in operand_kinds + out_kinds:
        if kind == "halves":
            made.append(Halves(refs.pop(0), refs.pop(0)))
        elif kind == "layer":
            made.append(Fetched(refs.pop(0).at[pl.ds(detail, 1)], mine.pop(0), mine.pop(0)))
        elif kind == "stored":
            made.append(Fetched(refs.pop(0), mine.pop(0), mine.pop(0)))
        elif kind == "saved":
            made.append(Saved(refs.pop(0), mine.pop(0), mine.pop(0), detail))
            saved.append(made[-1])
        else:
            made.append(refs.pop(0))
    kernel(*made, *refs)
    for out in saved:
        out.finish()


class Stored:
    def __init__(self, array):
        self.array = array


class Save:
    def __init__(self, shape, late=False):
        self.shape, self.late = shape, late


class Scalar:
    def __init__(self, array):
        self.array = array


SAVED_PIECES = 4


def run(kernel, operands, outs, flops, scratch=(), limit=LARGE):
    hbm = pltpu.MemorySpace.HBM
    specs, arrays, kinds, owned = [], [], [], []
    for operand in operands:
        if isinstance(operand, (tuple, Stored)):
            if isinstance(operand, Stored):
                array, number, shape = operand.array, None, operand.array.shape
                kinds.append(("stored", None))
            else:
                array, number = operand
                shape = (1,) + array.shape[1:]
                kinds.append(("layer", number))
            specs.append(pl.BlockSpec(memory_space=hbm))
            owned += [pltpu.VMEM(shape, array.dtype), pltpu.SemaphoreType.DMA(())]
            arrays.append(pltpu.with_memory_space_constraint(array, hbm))
        elif isinstance(operand, Scalar):
            kinds.append(("scalar", None))
            specs.append(pl.BlockSpec(memory_space=pltpu.SMEM))
            arrays.append(operand.array)
        elif isinstance(operand, list):
            kinds.append(("halves", None))
            specs += [whole()] * 2
            arrays += operand
        else:
            kinds.append(("whole", None))
            specs.append(whole())
            arrays.append(operand)
    shapes, out_kinds, out_specs = [], [], []
    for out in outs:
        if isinstance(out, list):
            out_kinds.append(("halves", None))
            shapes += [jax.ShapeDtypeStruct((out[0][0] // 2, out[0][1]), F32)] * 2
            out_specs += [whole()] * 2
        elif isinstance(out, Save):
            out_kinds.append(("saved", out.late))
            shapes.append(pltpu.MemorySpace.HBM(out.shape, F32))
            out_specs.append(pl.BlockSpec(memory_space=hbm))
            owned += [pltpu.VMEM(out.shape, F32), pltpu.SemaphoreType.DMA((SAVED_PIECES,))]
        else:
            out_kinds.append(("whole", None))
            shapes.append(jax.ShapeDtypeStruct(out, F32))
            out_specs.append(whole())
    results = list(
        pl.pallas_call(
            functools.partial(wrapped, kernel, kinds, out_kinds, len(owned)),
            out_shape=shapes,
            in_specs=specs,
            out_specs=out_specs,
            scratch_shapes=list(scratch) + owned,
            compiler_params=pltpu.CompilerParams(vmem_limit_bytes=limit * 2**20),
            cost_estimate=pl.CostEstimate(flops=flops, bytes_accessed=10**5, transcendentals=0),
        )(*arrays)
    )
    return [[results.pop(0), results.pop(0)] if kind == "halves" else results.pop(0) for kind, _ in out_kinds]


def bit_orders(count):
    bits = [1 << at for at in range(count.bit_length() - 1)]
    lead, rest = bits[:FLOWS], bits[FLOWS:]
    return [lead[at:] + lead[:at] for at in range(FLOWS)], rest


def block_masks(order):
    masks = [0]
    for bit in reversed(order):
        masks = masks + [mask + bit for mask in masks]
    return masks


def grad_kernel(mask_lists, permuted, pairs, top, me_ref, live_ref, *refs):
    ins, refs = refs[: 2 * len(pairs)], refs[2 * len(pairs):]
    outs, (turned_high, turned_low, high_ref, low_ref) = refs[: 2 * FLOWS], refs[2 * FLOWS:]
    depth = high_ref.shape[0]
    half = depth // 2
    starts = [0] * FLOWS
    for at, widths in enumerate(pairs):
        a_ref, b_ref = ins[2 * at], ins[2 * at + 1]
        if top:
            a_ref = Masked(a_ref, live_ref)
        if not permuted:
            turned_high[...], turned_low[...] = split_two(a_ref[...].T)
        for flow, masks in enumerate(mask_lists):
            if permuted:
                high_ref[...], low_ref[...] = split_two(a_ref[flow])
            else:
                rows = depth // len(masks)
                for place, mask in enumerate(masks):
                    source = pl.ds(pl.multiple_of((me_ref[0] ^ mask) * rows, 16), rows)
                    target = pl.ds(place * rows, rows)
                    high_ref[target, :] = turned_high[source, :]
                    low_ref[target, :] = turned_low[source, :]
            start, width, column = starts[flow], widths[flow], sum(widths[:flow])
            part_high, part_low = split_two(b_ref[:, column:column + width])
            for which in (1, 0):
                rows_at = pl.ds(which * half, half)
                outs[2 * flow + 1 - which][:, start:start + width] = (
                    product(high_ref[rows_at, :], part_high)
                    + product(high_ref[rows_at, :], part_low)
                    + product(low_ref[rows_at, :], part_high)
                )
            starts[flow] += width


def flow_widths(columns, shares):
    tiles = columns // LANES
    return tuple(LANES * (tiles * share // sum(shares)) for share in shares)


def grad_parts(pairs, names, me, live, count, top=False, shares=(1,) * FLOWS):
    orders, rest = bit_orders(count)
    mask_lists = [block_masks(order + rest) for order in orders]
    bare = [[one.array if isinstance(one, Stored) else one for one in two] for two in pairs]
    tokens, depth = bare[0][0].shape
    rows = depth // count
    permuted = rows % 16 != 0
    operands, widths = [Scalar(me.reshape(1)), Scalar(live)], []
    for (left, right), (left_array, right_array) in zip(pairs, bare):
        if permuted:
            if top:
                left_array = jnp.where(jnp.arange(tokens)[:, None] < live[0], left_array, 0.0)
            blocks = left_array.T.reshape(count, rows, tokens)
            left = jnp.stack(
                [jnp.take(blocks, me ^ jnp.array(masks, jnp.int32), axis=0).reshape(depth, tokens) for masks in mask_lists]
            )
        operands += [left, right]
        widths.append(flow_widths(right_array.shape[1], shares))
    outs = run(
        functools.partial(grad_kernel, mask_lists, permuted, widths, top and not permuted),
        operands, [(depth // 2, sum(one[flow] for one in widths)) for flow in range(FLOWS) for _ in range(2)], 10**6,
        [pltpu.VMEM((depth, tokens), BF16)] * 4,
    )
    parts = list(zip(names, widths))
    return {"send": outs[0::2], "keep": outs[1::2], "phase": 0, "parts": parts}


def fold_kernel(pieces, members, *refs):
    gots, keeps, outs = refs[: FLOWS * members], refs[FLOWS * members : 2 * FLOWS * members], refs[2 * FLOWS * members :]
    half = gots[0].shape[0] // 2
    for number, piece in enumerate(pieces):
        at = 0
        for flow in piece:
            for member in range(members):
                got, keep = gots[FLOWS * member + flow], keeps[FLOWS * member + flow]
                columns = slice(at, at + got.shape[1])
                at += got.shape[1]
                for which in (1, 0):
                    rows = slice(which * half, (which + 1) * half)
                    outs[len(pieces) * (1 - which) + number][:, columns] = got[rows, :] + keep[rows, :]


class Scatter:
    def __init__(self, count):
        self.count = count
        self.orders, self.rest = bit_orders(count)
        self.axes = [order[0] for order in self.orders]
        self.before, self.last = [], []
        self.rider = []
        self.flat, self.steps = None, self.rest + sorted(self.axes)

    def swap(self, values, bit):
        return lax.ppermute(values, "dp", [(one, one ^ bit) for one in range(self.count)])

    def launch(self, chunk, tokens=(), ride=None):
        gots, arrived = [None] * FLOWS, []
        for axis, bit in enumerate(self.axes):
            flow = [order[chunk["phase"]] for order in self.orders].index(bit)
            waits = list(tokens) + self.before + self.rider
            if self.last:
                waits.append(self.last[axis])
            (send,) = after([chunk["send"][flow]], waits)
            gots[flow] = self.swap(send, bit)
            arrived.append(gots[flow])
        chunk["got"] = gots
        if ride:
            self.ride(*ride)
        self.before, self.last = self.last, arrived

    def step(self):
        (send,) = after([self.flat], self.last)
        got = self.swap(send, self.steps.pop(0))
        self.flat = self.flat + got
        return got

    def ride(self, chunk, piece):
        (send,), keep = after([chunk["send"][piece]], self.before + self.rider), chunk["keep"][piece]
        for bit in self.rest[:-1]:
            total = keep + self.swap(send, bit)
            half = total.shape[0] // 2
            keep, send = total[:half], total[half:]
        got = self.swap(send, self.rest[-1])
        chunk["keep"][piece], chunk["got"][piece] = keep, got
        self.rider = [got]

    def fold(self, *chunks, pieces=tuple((flow,) for flow in range(FLOWS))):
        rows = chunks[0]["got"][0].shape[0]
        widths = [sum(chunk["got"][flow].shape[1] for chunk in chunks) for flow in range(FLOWS)]
        outs = [(rows // 2, sum(widths[flow] for flow in piece)) for piece in pieces] * 2
        operands = [got for chunk in chunks for got in chunk["got"]] + [keep for chunk in chunks for keep in chunk["keep"]]
        result = run(functools.partial(fold_kernel, pieces, len(chunks)), operands, outs, rows * sum(widths), limit=SMALL)
        return {
            "parts": [part for chunk in chunks for part in chunk["parts"]],
            "phase": chunks[0]["phase"] + 1,
            "pieces": pieces,
            "send": result[:len(pieces)],
            "keep": result[len(pieces):],
            "got": [None] * len(pieces),
        }


def pack_kernel(*refs):
    *terms, out_ref = refs
    at = 0
    for term in terms:
        for start in range(0, term.shape[1], LANES):
            out_ref[at:at + 1, :] = term[:, start:start + LANES]
            at += 1


def finish_kernel(layout, small, *refs):
    pairs = sum(len(pieces) for _, pieces in layout)
    keeps, gots, small_ref = refs[:pairs], refs[pairs:2 * pairs], refs[2 * pairs]
    out_ref, fc_ref, proj_ref, qkv_ref, *small_refs = refs[2 * pairs + 1:]
    number = 0
    for parts, pieces in layout:
        for piece in pieces:
            total = keeps[number][...] + gots[number][...]
            number += 1
            at = 0
            for flow in piece:
                for (name, layer), widths in parts:
                    column = sum(widths[:flow])
                    for start in range(0, widths[flow], LANES):
                        block = total[:, at + start:at + start + LANES]
                        member, place = divmod(column + start, qkv_ref.shape[-1])
                        if name == "qkv":
                            qkv_ref[layer, member, :, place:place + LANES] = block
                        else:
                            ref = {"out": out_ref, "fc": fc_ref, "proj": proj_ref}[name]
                            ref[layer, :, column + start:column + start + LANES] = block
                    at += widths[flow]
    at = 0
    for ref, (layers, size) in zip(small_refs, small):
        for layer in range(layers):
            for start in range(0, size, LANES):
                ref[layer:layer + 1, start:start + LANES] = small_ref[at:at + 1, :]
                at += 1


def after(values, tokens):
    if not tokens:
        return values
    return lax.optimization_barrier((values, list(tokens)))[0]


def on_device(
    count,
    pair,
    tokens,
    cotangent,
    doc_ids,
    live_rows,
    ln1_gain,
    ln1_shift,
    qkv_weight,
    qv_bias,
    proj_weight,
    proj_bias,
    ln2_gain,
    ln2_shift,
    fc_weight,
    fc_bias,
    out_weight,
    out_bias,
):
    row_count, depth = tokens.shape
    width, hidden = qkv_weight.shape[-1], fc_weight.shape[-1]
    top = qkv_weight.shape[0] - 1
    me = lax.axis_index("dp").astype(jnp.int32)
    model, half, wide, line = (row_count, depth), (row_count, width), (row_count, hidden), (1, depth)
    mask_scratch = pltpu.VMEM((row_count, row_count), F32)
    macs = row_count * depth * hidden
    live = Scalar(live_rows)
    groups = [Stored(doc_ids), live]
    ln1_gain, ln1_shift, ln2_gain, ln2_shift = Stored(ln1_gain), Stored(ln1_shift), Stored(ln2_gain), Stored(ln2_shift)
    qv_bias, proj_bias, fc_bias, out_bias = Stored(qv_bias), Stored(proj_bias), Stored(fc_bias), Stored(out_bias)

    def exchange(halves):
        return [lax.ppermute(part, "tensor", [(one, one ^ 1) for one in range(pair)]) for part in halves]

    stored = []
    entering = [Stored(tokens)]
    for number in range(top + 1):
        first = number == 0
        outs = [] if first else [Save(model)]
        outs += [Save(model), Save((row_count, 3 * width)), Save(half, late=True), Save((row_count, LANES), late=True), [model]]
        result = run(
            functools.partial(attend_kernel, number, first),
            entering + ([] if first else [out_bias])
            + [ln1_gain, ln1_shift, (qkv_weight, number), qv_bias, (proj_weight, number)] + groups,
            outs, 8 * macs, [mask_scratch],
        )
        stream = Stored(tokens if first else result[0])
        normed, qkv, mixed, logsum, branch = result[-5:]
        middle, normed_two, hidden_in, active, branch_two = run(
            functools.partial(mlp_kernel, number),
            [stream, branch, exchange(branch), proj_bias, ln2_gain, ln2_shift, (fc_weight, number), fc_bias, (out_weight, number)],
            [Save(model), Save(model), Save(wide), Save(wide), [model]], 8 * macs,
        )
        entering = [Stored(middle), branch_two, exchange(branch_two)]
        kept = (normed, qkv, mixed, logsum, middle, normed_two, hidden_in, active)
        stored.append((stream,) + tuple(Stored(array) for array in kept))

    scatter = Scatter(count)
    small = {}

    def mlp_back(number, operands, hidden_in):
        is_top = number == top
        outs = [] if is_top else [line, line, model]
        result = run(
            functools.partial(mlp_back_kernel, number, is_top),
            operands + [hidden_in, (fc_weight, number), (out_weight, number)],
            outs + [line, (1, hidden), wide, [model]], 24 * macs,
        )
        if is_top:
            grad = Stored(cotangent)
        else:
            small["ln1_gain", number + 1], small["ln1_shift", number + 1], grad = result[:3]
        small["out_bias", number], small["fc_bias", number], hidden_grad, branch = result[-4:]
        return grad, hidden_grad, branch

    def attend_back(number, grad, branch, got):
        stream, normed, qkv, mixed, logsum, middle = stored[number][:6]
        result = run(
            functools.partial(attend_back_kernel, number, number == top),
            [grad, middle, branch, got, ln2_gain, (proj_weight, number), (qkv_weight, number), qkv, mixed, logsum] + groups,
            [line, line, line, (1, 2 * width), model, (row_count, 3 * width), [model]], 32 * macs,
            [mask_scratch, pltpu.VMEM(half, F32)],
        )
        (small["ln2_gain", number], small["ln2_shift", number], small["proj_bias", number], small["qv_bias", number]) = result[:4]
        return result[4:]

    def out_parts(number, grad):
        return grad_parts([(grad, stored[number][8])], [("out", number)], me, live_rows, count, number == top)

    def fc_pair(number, hidden_grad):
        return (stored[number][6], hidden_grad), ("fc", number)

    def proj_pair(number, middle_grad):
        return (middle_grad, stored[number][3]), ("proj", number)

    def qkv_pair(number, qkv_grad):
        return (stored[number][1], qkv_grad), ("qkv", number)

    def parts_of(*named, shares=(1,) * FLOWS):
        return grad_parts([pair for pair, _ in named], [name for _, name in named], me, live_rows, count, shares=shares)

    grad, first_chunks = Stored(cotangent), None
    for number in reversed(range(top + 1)):
        if number == top:
            out_chunk = out_parts(number, grad)
            scatter.launch(out_chunk)
            (hidden_in,) = after([stored[number][7].array], out_chunk["keep"][:1])
            grad, hidden_grad, branch = mlp_back(number, [grad, live], Stored(hidden_in))
            got = exchange(branch)
            fc_chunk = parts_of(fc_pair(number, hidden_grad))
            scatter.launch(fc_chunk)
        else:
            above[:1] = after(above[:1], scatter.before)
            grad, hidden_grad, branch = mlp_back(number, above, stored[number][7])
            got = exchange(branch)
            out_chunk = out_parts(number, grad)
            scatter.launch(out_chunk, branch)
        got = after(got, scatter.before)
        middle_grad, qkv_grad, branch = attend_back(number, grad, branch, got)
        got = exchange(branch)
        if number == top:
            mix_chunk = parts_of(proj_pair(number, middle_grad), qkv_pair(number, qkv_grad))
            scatter.launch(mix_chunk)
            first_chunks = out_chunk, fc_chunk, mix_chunk
        else:
            first = scatter.fold(*first_chunks[:2])
            scatter.launch(first, branch)
            fc_chunk = parts_of(fc_pair(number, hidden_grad), proj_pair(number, middle_grad))
            scatter.launch(fc_chunk)
            mix_chunk = parts_of(qkv_pair(number, qkv_grad), shares=LAST_SHARES)
        above = [middle_grad, stored[number][0], branch, got, ln1_gain]
    gain_sum, shift_sum, input_grad = run(input_grad_kernel, above, [line, line, model], row_count * depth * 16)
    small["ln1_gain", 0], small["ln1_shift", 0] = gain_sum, shift_sum
    block_out = run(
        functools.partial(block_out_kernel, top), entering + [out_bias, live], [model], row_count * depth * 4
    )[0]
    names = ("ln1_gain", "ln1_shift", "qv_bias", "proj_bias", "ln2_gain", "ln2_shift", "fc_bias", "out_bias")
    terms = [small[name, number] for name in names for number in range(top + 1)]
    flat = run(pack_kernel, terms, [(sum(term.shape[1] for term in terms) // LANES, LANES)], 1000, limit=SMALL)[0]
    scatter.flat = flat

    two, one = ((0, 1), (2,)), ((0, 1, 2),)
    first = scatter.fold(first)
    scatter.launch(first, [flat, block_out])
    stepped = [scatter.step() for _ in scatter.rest][-1:]
    second = scatter.fold(first_chunks[2], out_chunk)
    first = scatter.fold(first, pieces=two)
    scatter.launch(second, ride=(first, 0))
    third = scatter.fold(fc_chunk)
    scatter.launch(third, stepped, ride=(first, 1))
    second = scatter.fold(second)
    scatter.launch(second)
    fourth = mix_chunk
    second = scatter.fold(second, pieces=two)
    scatter.launch(fourth, ride=(second, 0))
    third = scatter.fold(third)
    scatter.launch(third)
    fourth = scatter.fold(fourth)
    scatter.launch(fourth, ride=(second, 1))
    fourth, third = scatter.fold(fourth), scatter.fold(third, pieces=one)
    scatter.launch(fourth, ride=(third, 0))
    fourth = scatter.fold(fourth, pieces=one)
    scatter.rider = []
    scatter.ride(fourth, 0)
    while scatter.steps:
        scatter.step()
    chunks = (first, second, third, fourth)

    layers = top + 1
    rows = depth // count
    sizes = [(layers, small[name, 0].shape[1]) for name in names]
    result = run(
        functools.partial(finish_kernel, [(chunk["parts"], chunk["pieces"]) for chunk in chunks], sizes),
        [keep for chunk in chunks for keep in chunk["keep"]] + [got for chunk in chunks for got in chunk["got"]] + [scatter.flat],
        [(layers, rows, hidden), (layers, rows, hidden), (layers, rows, width), (layers, 3, rows, width)] + sizes,
        1000,
    )
    out_sum, fc_sum, proj_sum, qkv_sum, *sums = result
    ln1_gain_sum, ln1_shift_sum, qv_bias_sum, proj_bias_sum, ln2_gain_sum, ln2_shift_sum, fc_bias_sum, out_bias_sum = sums
    return (
        block_out,
        input_grad,
        ln1_gain_sum,
        ln1_shift_sum,
        qkv_sum,
        qv_bias_sum.reshape(layers, 2, width),
        proj_sum.transpose(0, 2, 1),
        proj_bias_sum,
        ln2_gain_sum,
        ln2_shift_sum,
        fc_sum,
        fc_bias_sum,
        out_sum.transpose(0, 2, 1),
        out_bias_sum,
    )


def solution(mesh):
    in_specs = (
        P("dp", None),
        P("dp", None),
        P("dp", None),
        P("dp"),
        P(),
        P(),
        P(None, None, None, "tensor"),
        P(None, None, "tensor"),
        P(None, "tensor", None),
        P(),
        P(),
        P(),
        P(None, None, "tensor"),
        P(None, "tensor"),
        P(None, "tensor", None),
        P(),
    )
    out_specs = (
        P("dp", None),
        P("dp", None),
        P(),
        P(),
        P(None, None, "dp", "tensor"),
        P(None, None, "tensor"),
        P(None, "tensor", "dp"),
        P(),
        P(),
        P(),
        P(None, "dp", "tensor"),
        P(None, "tensor"),
        P(None, "tensor", "dp"),
        P(),
    )
    return jax.shard_map(
        functools.partial(on_device, mesh.shape["dp"], mesh.shape["tensor"]),
        mesh=mesh,
        in_specs=in_specs,
        out_specs=out_specs,
        check_vma=False,
    )
```

```python
import functools

import jax
import jax.numpy as jnp
from jax import lax
from jax.experimental import pallas as pl
from jax.experimental.pallas import tpu as pltpu
from jax.sharding import PartitionSpec as P

HEAD_DIM = 64
EPSILON = 1e-05
LANES = 128
HEAD_SCALE = HEAD_DIM ** (-0.5)
MASKED = -1e30
F32 = jnp.float32
BF16 = jnp.bfloat16
GELU_A = 0.7978845608028654
GELU_B = 0.044715
HIDDEN_TILE = 512
FLOWS = 3
LARGE = 24
LAST_SHARES = (4, 3, 2)
SMALL = 16
ROW_BLOCK = 384


def split_two(values):
    high = values.astype(BF16)
    return high, (values - high.astype(F32)).astype(BF16)


def product(left, right):
    return jnp.dot(left, right, preferred_element_type=F32)


def product_turned(left, right):
    return lax.dot_general(left, right, (((1,), (1,)), ((), ())), preferred_element_type=F32)


def turned_product(left, right):
    return lax.dot_general(left, right, (((0,), (0,)), ((), ())), preferred_element_type=F32)


def by_weight(pair, weight):
    return product(pair[0], weight) + product(pair[1], weight)


def by_weight_turned(pair, weight):
    return product_turned(pair[0], weight) + product_turned(pair[1], weight)


def normalize(values):
    centred = values - jnp.mean(values, axis=-1, keepdims=True)
    scale = lax.rsqrt(jnp.mean(centred * centred, axis=-1, keepdims=True) + EPSILON)
    return centred * scale, scale


def norm_backward(grad, unit, scale, norm_gain):
    gained = grad * norm_gain
    mean_grad = jnp.mean(gained, axis=-1, keepdims=True)
    mean_dot = jnp.mean(gained * unit, axis=-1, keepdims=True)
    return scale * (gained - mean_grad - unit * mean_dot)


def column_sum(values):
    return jnp.sum(values, axis=0, keepdims=True)


def gelu(values):
    bent = jnp.tanh(GELU_A * (values + GELU_B * values * values * values))
    return 0.5 * values * (1.0 + bent)


def gelu_slope(values):
    square = values * values
    bent = jnp.tanh(GELU_A * (values + GELU_B * values * square))
    inner = GELU_A * (1.0 + 3.0 * GELU_B * square)
    return 0.5 * (1.0 + bent) + 0.5 * values * (1.0 - bent * bent) * inner


def fill_mask(mask_ref, doc_ref, live_ref):
    shape = mask_ref.shape
    position = lax.broadcasted_iota(jnp.int32, (8, shape[1]), 1)
    documents = jnp.broadcast_to(doc_ref[...], (8, shape[1]))
    tags = jnp.where(position < live_ref[0], documents, -1).astype(F32)
    same = tags.T[:, :1] == tags[:1, :]
    causal = lax.broadcasted_iota(jnp.int32, shape, 1) <= lax.broadcasted_iota(jnp.int32, shape, 0)
    mask_ref[...] = jnp.where(same & causal, 1.0, 0.0)


def living(shape, live_ref):
    return jnp.where(lax.broadcasted_iota(jnp.int32, shape, 0) < live_ref[0], 1.0, 0.0)


def attend_kernel(number, first, *refs):
    if first:
        x_ref, *refs = refs
        values = x_ref[...]
    else:
        m_ref, part_ref, got_ref, out_bias_ref, *refs = refs
        values = m_ref[...] + (part_ref[...] + got_ref[...]) + out_bias_ref[number - 1:number, :]
    gain_ref, shift_ref, weight_ref, bias_ref, proj_ref, doc_ref, live_ref, *refs = refs
    if not first:
        x_out_ref, *refs = refs
        x_out_ref[...] = values
    normed_ref, qkv_ref, result_ref, logsum_ref, branch_ref, mask_ref = refs
    rows = values.shape[0]
    unit, _ = normalize(values)
    normed = unit * gain_ref[number:number + 1, :] + shift_ref[number:number + 1, :]
    normed_ref[...] = normed
    pair = split_two(normed)
    width = weight_ref.shape[-1]
    for member in range(3):
        piece = by_weight(pair, weight_ref[0, member])
        if member != 1:
            piece = piece + bias_ref[number, member // 2:member // 2 + 1, :]
        qkv_ref[:, member * width:(member + 1) * width] = piece
    fill_mask(mask_ref, doc_ref, live_ref)
    for head in range(width // HEAD_DIM):
        low_at = head * HEAD_DIM
        query, key, value = (
            split_two(qkv_ref[:, member * width + low_at:member * width + low_at + HEAD_DIM]) for member in range(3)
        )
        queries = jnp.concatenate([query[0], query[0], query[1]], axis=1)
        keys = jnp.concatenate([key[0], key[1], key[0]], axis=1)
        both = jnp.concatenate([value[0], value[1]], axis=1)
        for start in range(0, rows, ROW_BLOCK):
            stop = start + ROW_BLOCK
            scores = product_turned(queries[start:stop], keys[:stop]) * HEAD_SCALE
            scores = jnp.where(mask_ref[start:stop, :stop] > 0.5, scores, MASKED)
            peak = jnp.max(scores, axis=1, keepdims=True)
            weights = jnp.exp(scores - peak)
            total = jnp.sum(weights, axis=1, keepdims=True)
            logsum_ref[start:stop, head:head + 1] = peak + jnp.log(total)
            high, low = split_two(weights)
            mixed = product(high, both[:stop])
            mixed = mixed[:, :HEAD_DIM] + mixed[:, HEAD_DIM:] + product(low, value[0][:stop])
            result_ref[start:stop, low_at:low_at + HEAD_DIM] = mixed / total
    branch_ref[...] = by_weight(split_two(result_ref[...]), proj_ref[0])


def mlp_kernel(
    number, x_ref, part_ref, got_ref, proj_bias_ref, gain_ref, shift_ref, fc_ref, fc_bias_ref, out_ref,
    middle_ref, normed_ref, hidden_ref, active_ref, branch_ref,
):
    values = x_ref[...] + (part_ref[...] + got_ref[...]) + proj_bias_ref[number:number + 1, :]
    middle_ref[...] = values
    unit, _ = normalize(values)
    normed = unit * gain_ref[number:number + 1, :] + shift_ref[number:number + 1, :]
    normed_ref[...] = normed
    pair = split_two(normed)
    tiles = [slice(start, start + HIDDEN_TILE) for start in range(0, fc_ref.shape[-1], HIDDEN_TILE)]
    entered = lambda tile: by_weight(pair, fc_ref[0, :, tile]) + fc_bias_ref[number:number + 1, tile]
    total, hidden = None, entered(tiles[0])
    for at, tile in enumerate(tiles):
        later = entered(tiles[at + 1]) if at + 1 < len(tiles) else None
        active = gelu(hidden)
        term = by_weight(split_two(active), out_ref[0, tile, :])
        total = term if total is None else total + term
        hidden_ref[:, tile], active_ref[:, tile] = hidden, active
        hidden = later
    branch_ref[...] = total


def stream_grad(number, grad_ref, x_ref, part_ref, got_ref, gain_ref, gain_sum_ref, shift_sum_ref):
    unit, scale = normalize(x_ref[...])
    arriving = part_ref[...] + got_ref[...]
    gain_sum_ref[...] = column_sum(arriving * unit)
    shift_sum_ref[...] = column_sum(arriving)
    return grad_ref[...] + norm_backward(arriving, unit, scale, gain_ref[number:number + 1, :])


def mlp_back_kernel(number, top, *refs):
    if top:
        cotangent_ref, live_ref, *refs = refs
    else:
        above, refs = refs[:5], refs[5:]
    hidden_ref, fc_ref, out_ref, *refs = refs
    if top:
        grad = Masked(cotangent_ref, live_ref)[...]
    else:
        gain_sum_ref, shift_sum_ref, grad_ref, *refs = refs
        grad = stream_grad(number + 1, *above, gain_sum_ref, shift_sum_ref)
        grad_ref[...] = grad
    out_bias_ref, fc_bias_ref, hidden_grad_ref, branch_ref = refs
    out_bias_ref[...] = column_sum(grad)
    pair = split_two(grad)
    tiles = [slice(start, start + HIDDEN_TILE) for start in range(0, fc_ref.shape[-1], HIDDEN_TILE)]
    total, active_grad = None, by_weight_turned(pair, out_ref[0, tiles[0], :])
    for at, tile in enumerate(tiles):
        later = by_weight_turned(pair, out_ref[0, tiles[at + 1], :]) if at + 1 < len(tiles) else None
        hidden_grad = gelu_slope(hidden_ref[:, tile]) * active_grad
        active_grad = later
        hidden_grad_ref[:, tile] = hidden_grad
        fc_bias_ref[:, tile] = column_sum(hidden_grad)
        term = by_weight_turned(split_two(hidden_grad), fc_ref[0, :, tile])
        total = term if total is None else total + term
    branch_ref[...] = total


def attend_back_kernel(
    number, top, grad_ref, middle_ref, part_ref, got_ref, gain_ref, proj_ref, weight_ref, qkv_ref, result_ref, logsum_ref,
    doc_ref, live_ref,
    gain_sum_ref, shift_sum_ref, proj_bias_ref, bias_ref, middle_grad_ref, qkv_grad_ref, branch_ref,
    mask_ref, result_grad_ref,
):
    if top:
        grad_ref = Masked(grad_ref, live_ref)
    grad = stream_grad(number, grad_ref, middle_ref, part_ref, got_ref, gain_ref, gain_sum_ref, shift_sum_ref)
    middle_grad_ref[...] = grad
    proj_bias_ref[...] = column_sum(grad)
    result_grad_ref[...] = by_weight_turned(split_two(grad), proj_ref[0])
    fill_mask(mask_ref, doc_ref, live_ref)
    rows, width = result_ref.shape
    for head in range(width // HEAD_DIM):
        low_at = head * HEAD_DIM
        columns = slice(low_at, low_at + HEAD_DIM)
        query, key, value = (
            split_two(qkv_ref[:, member * width + low_at:member * width + low_at + HEAD_DIM]) for member in range(3)
        )
        given = result_grad_ref[:, columns]
        given_pair = split_two(given)
        delta = jnp.sum(given * result_ref[:, columns], axis=1, keepdims=True)
        queries = jnp.concatenate([query[0], query[0], query[1]], axis=1)
        keys = jnp.concatenate([key[0], key[1], key[0]], axis=1)
        givens = jnp.concatenate([given_pair[0], given_pair[0], given_pair[1]], axis=1)
        values = jnp.concatenate([value[0], value[1], value[0]], axis=1)
        key_both = jnp.concatenate([key[0], key[1]], axis=1)
        query_both = jnp.concatenate([query[0], query[1]], axis=1)
        given_both = jnp.concatenate([given_pair[0], given_pair[1]], axis=1)
        for start in range(0, rows, ROW_BLOCK):
            stop = start + ROW_BLOCK
            scores = product_turned(queries[start:stop], keys[:stop]) * HEAD_SCALE
            scores = jnp.where(mask_ref[start:stop, :stop] > 0.5, scores, MASKED)
            weights = jnp.exp(scores - logsum_ref[start:stop, head:head + 1])
            weights_grad = product_turned(givens[start:stop], values[:stop])
            scores_grad = weights * (weights_grad - delta[start:stop]) * HEAD_SCALE
            high, low = split_two(scores_grad)
            mixed = product(high, key_both[:stop])
            qkv_grad_ref[start:stop, columns] = (
                mixed[:, :HEAD_DIM] + mixed[:, HEAD_DIM:] + product(low, key[0][:stop])
            )
            mixed = turned_product(high, query_both[start:stop])
            key_grad = mixed[:, :HEAD_DIM] + mixed[:, HEAD_DIM:] + turned_product(low, query[0][start:stop])
            high, low = split_two(weights)
            mixed = turned_product(high, given_both[start:stop])
            value_grad = mixed[:, :HEAD_DIM] + mixed[:, HEAD_DIM:] + turned_product(low, given_pair[0][start:stop])
            for member, term in ((1, key_grad), (2, value_grad)):
                at = slice(member * width + low_at, member * width + low_at + HEAD_DIM)
                if start == 0:
                    qkv_grad_ref[:stop, at] = term
                else:
                    qkv_grad_ref[:start, at] += term[:start]
                    qkv_grad_ref[start:stop, at] = term[start:]
    total = None
    for member in range(3):
        piece = qkv_grad_ref[:, member * width:(member + 1) * width]
        if member != 1:
            bias_ref[:, (member // 2) * width:(member // 2 + 1) * width] = column_sum(piece)
        term = by_weight_turned(split_two(piece), weight_ref[0, member])
        total = term if total is None else total + term
    branch_ref[...] = total


def input_grad_kernel(grad_ref, x_ref, part_ref, got_ref, gain_ref, gain_sum_ref, shift_sum_ref, out_ref):
    out_ref[...] = stream_grad(0, grad_ref, x_ref, part_ref, got_ref, gain_ref, gain_sum_ref, shift_sum_ref)


def block_out_kernel(number, middle_ref, part_ref, got_ref, out_bias_ref, live_ref, out_ref):
    values = middle_ref[...] + (part_ref[...] + got_ref[...]) + out_bias_ref[number:number + 1, :]
    out_ref[...] = values * living(values.shape, live_ref)


def whole():
    return pl.BlockSpec(memory_space=pltpu.VMEM)


class Fetched:
    def __init__(self, source, target, semaphore):
        self.copy = pltpu.make_async_copy(source, target, semaphore)
        self.copy.start()
        self.target = target
        self.shape = target.shape
        self.waiting = True

    def __getitem__(self, index):
        if self.waiting:
            self.copy.wait()
            self.waiting = False
        return self.target[index]


class Masked:
    def __init__(self, ref, live_ref):
        self.ref, self.live_ref, self.shape = ref, live_ref, ref.shape

    def __getitem__(self, index):
        return self.ref[index] * living(self.shape, self.live_ref)


class Saved:
    def __init__(self, target, stage, semaphores, late):
        self.target, self.stage, self.semaphores, self.late = target, stage, semaphores, late
        self.shape, self.copies = stage.shape, []

    def push(self, index):
        source, target = self.stage.at[index], self.target.at[index]
        self.copies.append(pltpu.make_async_copy(source, target, self.semaphores.at[len(self.copies)]))
        self.copies[-1].start()

    def __getitem__(self, index):
        return self.stage[index]

    def __setitem__(self, index, values):
        self.stage[index] = values
        if not self.late:
            self.push(index)

    def finish(self):
        if self.late:
            self.push(Ellipsis)
        for copy in self.copies:
            copy.wait()


class Halves:
    def __init__(self, upper, lower):
        self.refs = upper, lower

    def __getitem__(self, index):
        return jnp.concatenate([ref[...] for ref in self.refs], axis=0)

    def __setitem__(self, index, values):
        rows = values.shape[0] // 2
        self.refs[0][...], self.refs[1][...] = values[:rows], values[rows:]


def wrapped(kernel, operand_kinds, out_kinds, owned, *refs):
    refs = list(refs)
    mine, refs = refs[len(refs) - owned:], refs[:len(refs) - owned]
    made, saved = [], []
    for kind, detail in operand_kinds + out_kinds:
        if kind == "halves":
            made.append(Halves(refs.pop(0), refs.pop(0)))
        elif kind == "layer":
            made.append(Fetched(refs.pop(0).at[pl.ds(detail, 1)], mine.pop(0), mine.pop(0)))
        elif kind == "stored":
            made.append(Fetched(refs.pop(0), mine.pop(0), mine.pop(0)))
        elif kind == "saved":
            made.append(Saved(refs.pop(0), mine.pop(0), mine.pop(0), detail))
            saved.append(made[-1])
        else:
            made.append(refs.pop(0))
    kernel(*made, *refs)
    for out in saved:
        out.finish()


class Stored:
    def __init__(self, array):
        self.array = array


class Save:
    def __init__(self, shape, late=False):
        self.shape, self.late = shape, late


class Scalar:
    def __init__(self, array):
        self.array = array


SAVED_PIECES = 4


def run(kernel, operands, outs, flops, scratch=(), limit=LARGE):
    hbm = pltpu.MemorySpace.HBM
    specs, arrays, kinds, owned = [], [], [], []
    for operand in operands:
        if isinstance(operand, (tuple, Stored)):
            if isinstance(operand, Stored):
                array, number, shape = operand.array, None, operand.array.shape
                kinds.append(("stored", None))
            else:
                array, number = operand
                shape = (1,) + array.shape[1:]
                kinds.append(("layer", number))
            specs.append(pl.BlockSpec(memory_space=hbm))
            owned += [pltpu.VMEM(shape, array.dtype), pltpu.SemaphoreType.DMA(())]
            arrays.append(pltpu.with_memory_space_constraint(array, hbm))
        elif isinstance(operand, Scalar):
            kinds.append(("scalar", None))
            specs.append(pl.BlockSpec(memory_space=pltpu.SMEM))
            arrays.append(operand.array)
        elif isinstance(operand, list):
            kinds.append(("halves", None))
            specs += [whole()] * 2
            arrays += operand
        else:
            kinds.append(("whole", None))
            specs.append(whole())
            arrays.append(operand)
    shapes, out_kinds, out_specs = [], [], []
    for out in outs:
        if isinstance(out, list):
            out_kinds.append(("halves", None))
            shapes += [jax.ShapeDtypeStruct((out[0][0] // 2, out[0][1]), F32)] * 2
            out_specs += [whole()] * 2
        elif isinstance(out, Save):
            out_kinds.append(("saved", out.late))
            shapes.append(pltpu.MemorySpace.HBM(out.shape, F32))
            out_specs.append(pl.BlockSpec(memory_space=hbm))
            owned += [pltpu.VMEM(out.shape, F32), pltpu.SemaphoreType.DMA((SAVED_PIECES,))]
        else:
            out_kinds.append(("whole", None))
            shapes.append(jax.ShapeDtypeStruct(out, F32))
            out_specs.append(whole())
    results = list(
        pl.pallas_call(
            functools.partial(wrapped, kernel, kinds, out_kinds, len(owned)),
            out_shape=shapes,
            in_specs=specs,
            out_specs=out_specs,
            scratch_shapes=list(scratch) + owned,
            compiler_params=pltpu.CompilerParams(vmem_limit_bytes=limit * 2**20),
            cost_estimate=pl.CostEstimate(flops=flops, bytes_accessed=10**5, transcendentals=0),
        )(*arrays)
    )
    return [[results.pop(0), results.pop(0)] if kind == "halves" else results.pop(0) for kind, _ in out_kinds]


def bit_orders(count):
    bits = [1 << at for at in range(count.bit_length() - 1)]
    lead, rest = bits[:FLOWS], bits[FLOWS:]
    return [lead[at:] + lead[:at] for at in range(FLOWS)], rest


def block_masks(order):
    masks = [0]
    for bit in reversed(order):
        masks = masks + [mask + bit for mask in masks]
    return masks


def grad_kernel(mask_lists, permuted, pairs, top, halves, me_ref, live_ref, *refs):
    ins, refs = refs[: 2 * len(pairs)], refs[2 * len(pairs):]
    outs, (turned_high, turned_low, high_ref, low_ref) = refs[: len(halves) * FLOWS], refs[len(halves) * FLOWS:]
    depth = high_ref.shape[0]
    half = depth // 2
    starts = [0] * FLOWS
    for at, widths in enumerate(pairs):
        a_ref, b_ref = ins[2 * at], ins[2 * at + 1]
        if top:
            a_ref = Masked(a_ref, live_ref)
        if not permuted:
            turned_high[...], turned_low[...] = split_two(a_ref[...].T)
        for flow, masks in enumerate(mask_lists):
            if permuted:
                high_ref[...], low_ref[...] = split_two(a_ref[flow])
            else:
                rows = depth // len(masks)
                for place, mask in enumerate(masks):
                    if place // (len(masks) // 2) not in halves:
                        continue
                    source = pl.ds(pl.multiple_of((me_ref[0] ^ mask) * rows, 16), rows)
                    target = pl.ds(place * rows, rows)
                    high_ref[target, :] = turned_high[source, :]
                    low_ref[target, :] = turned_low[source, :]
            start, width, column = starts[flow], widths[flow], sum(widths[:flow])
            part_high, part_low = split_two(b_ref[:, column:column + width])
            for place, which in enumerate(halves):
                rows_at = pl.ds(which * half, half)
                outs[len(halves) * flow + place][:, start:start + width] = (
                    product(high_ref[rows_at, :], part_high)
                    + product(high_ref[rows_at, :], part_low)
                    + product(low_ref[rows_at, :], part_high)
                )
            starts[flow] += width


def flow_widths(columns, shares):
    tiles = columns // LANES
    return tuple(LANES * (tiles * share // sum(shares)) for share in shares)


def grad_parts(pairs, names, me, live, count, top=False, shares=(1,) * FLOWS, sends_first=False):
    orders, rest = bit_orders(count)
    mask_lists = [block_masks(order + rest) for order in orders]
    bare = [[one.array if isinstance(one, Stored) else one for one in two] for two in pairs]
    tokens, depth = bare[0][0].shape
    rows = depth // count
    permuted = rows % 16 != 0
    operands, widths = [Scalar(me.reshape(1)), Scalar(live)], []
    for (left, right), (left_array, right_array) in zip(pairs, bare):
        if permuted:
            if top:
                left_array = jnp.where(jnp.arange(tokens)[:, None] < live[0], left_array, 0.0)
            blocks = left_array.T.reshape(count, rows, tokens)
            left = jnp.stack(
                [jnp.take(blocks, me ^ jnp.array(masks, jnp.int32), axis=0).reshape(depth, tokens) for masks in mask_lists]
            )
        operands += [left, right]
        widths.append(flow_widths(right_array.shape[1], shares))
    def halves_of(*halves):
        outs = [(depth // 2, sum(one[flow] for one in widths)) for flow in range(FLOWS) for _ in halves]
        kernel = functools.partial(grad_kernel, mask_lists, permuted, widths, top and not permuted, halves)
        return run(kernel, operands, outs, 10**6, [pltpu.VMEM((depth, tokens), BF16)] * 4)

    if sends_first:
        sends, keeps = halves_of(1), halves_of(0)
    else:
        both = halves_of(1, 0)
        sends, keeps = both[0::2], both[1::2]
    return {"send": sends, "keep": keeps, "phase": 0, "parts": list(zip(names, widths))}


def fold_kernel(pieces, members, *refs):
    gots, keeps, outs = refs[: FLOWS * members], refs[FLOWS * members : 2 * FLOWS * members], refs[2 * FLOWS * members :]
    half = gots[0].shape[0] // 2
    for number, piece in enumerate(pieces):
        at = 0
        for flow in piece:
            for member in range(members):
                got, keep = gots[FLOWS * member + flow], keeps[FLOWS * member + flow]
                columns = slice(at, at + got.shape[1])
                at += got.shape[1]
                for which in (1, 0):
                    rows = slice(which * half, (which + 1) * half)
                    outs[len(pieces) * (1 - which) + number][:, columns] = got[rows, :] + keep[rows, :]


class Scatter:
    def __init__(self, count):
        self.count = count
        self.orders, self.rest = bit_orders(count)
        self.axes = [order[0] for order in self.orders]
        self.before, self.last = [], []
        self.rider = []
        self.flat, self.steps = None, self.rest + sorted(self.axes)

    def swap(self, values, bit):
        return lax.ppermute(values, "dp", [(one, one ^ bit) for one in range(self.count)])

    def launch(self, chunk, tokens=(), ride=None, step=False, early=False):
        gots, arrived = [None] * FLOWS, []
        for axis, bit in enumerate(self.axes):
            flow = [order[chunk["phase"]] for order in self.orders].index(bit)
            waits = list(tokens) + self.before
            if early and axis == FLOWS - 1:
                (send,) = after([chunk["send"][flow]], waits)
                gots[flow] = self.swap(send, bit)
                arrived.append(gots[flow])
                continue
            waits += self.rider
            if self.last:
                waits.append(self.last[axis])
            (send,) = after([chunk["send"][flow]], waits)
            gots[flow] = self.swap(send, bit)
            arrived.append(gots[flow])
        chunk["got"] = gots
        if ride:
            self.ride(*ride)
        if step:
            self.rider = self.rider + [self.step()]
        self.before, self.last = self.last, arrived

    def step(self):
        (send,) = after([self.flat], self.last)
        got = self.swap(send, self.steps.pop(0))
        self.flat = self.flat + got
        return got

    def ride(self, chunk, piece):
        (send,), keep = after([chunk["send"][piece]], self.before + self.rider), chunk["keep"][piece]
        for bit in self.rest[:-1]:
            total = keep + self.swap(send, bit)
            half = total.shape[0] // 2
            keep, send = total[:half], total[half:]
        got = self.swap(send, self.rest[-1])
        chunk["keep"][piece], chunk["got"][piece] = keep, got
        self.rider = [got]

    def fold(self, *chunks, pieces=tuple((flow,) for flow in range(FLOWS))):
        rows = chunks[0]["got"][0].shape[0]
        widths = [sum(chunk["got"][flow].shape[1] for chunk in chunks) for flow in range(FLOWS)]
        outs = [(rows // 2, sum(widths[flow] for flow in piece)) for piece in pieces] * 2
        operands = [got for chunk in chunks for got in chunk["got"]] + [keep for chunk in chunks for keep in chunk["keep"]]
        result = run(functools.partial(fold_kernel, pieces, len(chunks)), operands, outs, rows * sum(widths), limit=SMALL)
        return {
            "parts": [part for chunk in chunks for part in chunk["parts"]],
            "phase": chunks[0]["phase"] + 1,
            "pieces": pieces,
            "send": result[:len(pieces)],
            "keep": result[len(pieces):],
            "got": [None] * len(pieces),
        }


def pack_kernel(*refs):
    *terms, out_ref = refs
    at = 0
    for term in terms:
        for start in range(0, term.shape[1], LANES):
            out_ref[at:at + 1, :] = term[:, start:start + LANES]
            at += 1


def finish_kernel(layout, small, *refs):
    pairs = sum(len(pieces) for _, pieces in layout)
    keeps, gots, small_ref = refs[:pairs], refs[pairs:2 * pairs], refs[2 * pairs]
    out_ref, fc_ref, proj_ref, qkv_ref, *small_refs = refs[2 * pairs + 1:]
    number = 0
    for parts, pieces in layout:
        for piece in pieces:
            total = keeps[number][...] + gots[number][...]
            number += 1
            at = 0
            for flow in piece:
                for (name, layer), widths in parts:
                    column = sum(widths[:flow])
                    for start in range(0, widths[flow], LANES):
                        block = total[:, at + start:at + start + LANES]
                        member, place = divmod(column + start, qkv_ref.shape[-1])
                        if name == "qkv":
                            qkv_ref[layer, member, :, place:place + LANES] = block
                        else:
                            ref = {"out": out_ref, "fc": fc_ref, "proj": proj_ref}[name]
                            ref[layer, :, column + start:column + start + LANES] = block
                    at += widths[flow]
    at = 0
    for ref, (layers, size) in zip(small_refs, small):
        for layer in range(layers):
            for start in range(0, size, LANES):
                ref[layer:layer + 1, start:start + LANES] = small_ref[at:at + 1, :]
                at += 1


def after(values, tokens):
    if not tokens:
        return values
    return lax.optimization_barrier((values, list(tokens)))[0]


def on_device(
    count,
    pair,
    tokens,
    cotangent,
    doc_ids,
    live_rows,
    ln1_gain,
    ln1_shift,
    qkv_weight,
    qv_bias,
    proj_weight,
    proj_bias,
    ln2_gain,
    ln2_shift,
    fc_weight,
    fc_bias,
    out_weight,
    out_bias,
):
    row_count, depth = tokens.shape
    width, hidden = qkv_weight.shape[-1], fc_weight.shape[-1]
    top = qkv_weight.shape[0] - 1
    me = lax.axis_index("dp").astype(jnp.int32)
    model, half, wide, line = (row_count, depth), (row_count, width), (row_count, hidden), (1, depth)
    mask_scratch = pltpu.VMEM((row_count, row_count), F32)
    macs = row_count * depth * hidden
    live = Scalar(live_rows)
    groups = [Stored(doc_ids), live]
    ln1_gain, ln1_shift, ln2_gain, ln2_shift = Stored(ln1_gain), Stored(ln1_shift), Stored(ln2_gain), Stored(ln2_shift)
    qv_bias, proj_bias, fc_bias, out_bias = Stored(qv_bias), Stored(proj_bias), Stored(fc_bias), Stored(out_bias)

    def exchange(halves):
        return [lax.ppermute(part, "tensor", [(one, one ^ 1) for one in range(pair)]) for part in halves]

    stored = []
    entering = [Stored(tokens)]
    for number in range(top + 1):
        first = number == 0
        outs = [] if first else [Save(model)]
        outs += [Save(model), Save((row_count, 3 * width)), Save(half, late=True), Save((row_count, LANES), late=True), [model]]
        result = run(
            functools.partial(attend_kernel, number, first),
            entering + ([] if first else [out_bias])
            + [ln1_gain, ln1_shift, (qkv_weight, number), qv_bias, (proj_weight, number)] + groups,
            outs, 8 * macs, [mask_scratch],
        )
        stream = Stored(tokens if first else result[0])
        normed, qkv, mixed, logsum, branch = result[-5:]
        middle, normed_two, hidden_in, active, branch_two = run(
            functools.partial(mlp_kernel, number),
            [stream, branch, exchange(branch), proj_bias, ln2_gain, ln2_shift, (fc_weight, number), fc_bias, (out_weight, number)],
            [Save(model), Save(model), Save(wide), Save(wide), [model]], 8 * macs,
        )
        entering = [Stored(middle), branch_two, exchange(branch_two)]
        kept = (normed, qkv, mixed, logsum, middle, normed_two, hidden_in, active)
        stored.append((stream,) + tuple(Stored(array) for array in kept))

    scatter = Scatter(count)
    small = {}

    def mlp_back(number, operands, hidden_in):
        is_top = number == top
        outs = [] if is_top else [line, line, model]
        result = run(
            functools.partial(mlp_back_kernel, number, is_top),
            operands + [hidden_in, (fc_weight, number), (out_weight, number)],
            outs + [line, (1, hidden), wide, [model]], 24 * macs,
        )
        if is_top:
            grad = Stored(cotangent)
        else:
            small["ln1_gain", number + 1], small["ln1_shift", number + 1], grad = result[:3]
        small["out_bias", number], small["fc_bias", number], hidden_grad, branch = result[-4:]
        return grad, hidden_grad, branch

    def attend_back(number, grad, branch, got):
        stream, normed, qkv, mixed, logsum, middle = stored[number][:6]
        result = run(
            functools.partial(attend_back_kernel, number, number == top),
            [grad, middle, branch, got, ln2_gain, (proj_weight, number), (qkv_weight, number), qkv, mixed, logsum] + groups,
            [line, line, line, (1, 2 * width), model, (row_count, 3 * width), [model]], 32 * macs,
            [mask_scratch, pltpu.VMEM(half, F32)],
        )
        (small["ln2_gain", number], small["ln2_shift", number], small["proj_bias", number], small["qv_bias", number]) = result[:4]
        return result[4:]

    def out_parts(number, grad):
        return grad_parts([(grad, stored[number][8])], [("out", number)], me, live_rows, count, number == top, sends_first=number == top)

    def fc_pair(number, hidden_grad):
        return (stored[number][6], hidden_grad), ("fc", number)

    def proj_pair(number, middle_grad):
        return (middle_grad, stored[number][3]), ("proj", number)

    def qkv_pair(number, qkv_grad):
        return (stored[number][1], qkv_grad), ("qkv", number)

    def parts_of(*named, **options):
        return grad_parts([pair for pair, _ in named], [name for _, name in named], me, live_rows, count, **options)

    grad, first_chunks = Stored(cotangent), None
    for number in reversed(range(top + 1)):
        if number == top:
            out_chunk = out_parts(number, grad)
            scatter.launch(out_chunk)
            (hidden_in,) = after([stored[number][7].array], out_chunk["send"][:1])
            grad, hidden_grad, branch = mlp_back(number, [grad, live], Stored(hidden_in))
            got = exchange(branch)
            fc_chunk = parts_of(fc_pair(number, hidden_grad))
            scatter.launch(fc_chunk)
        else:
            above[:1] = after(above[:1], scatter.before)
            grad, hidden_grad, branch = mlp_back(number, above, stored[number][7])
            got = exchange(branch)
            out_chunk = out_parts(number, grad)
            scatter.launch(out_chunk, branch)
        got = after(got, scatter.before)
        middle_grad, qkv_grad, branch = attend_back(number, grad, branch, got)
        got = exchange(branch)
        if number == top:
            mix_chunk = parts_of(proj_pair(number, middle_grad), qkv_pair(number, qkv_grad), sends_first=True)
            scatter.launch(mix_chunk)
            first_chunks = out_chunk, fc_chunk, mix_chunk
        else:
            first = scatter.fold(*first_chunks[:2])
            scatter.launch(first, branch)
            fc_chunk = parts_of(fc_pair(number, hidden_grad), proj_pair(number, middle_grad))
            scatter.launch(fc_chunk, first_chunks[2]["keep"][:1])
            mix_chunk = parts_of(qkv_pair(number, qkv_grad), shares=LAST_SHARES)
        above = [middle_grad, stored[number][0], branch, got, ln1_gain]
    gain_sum, shift_sum, input_grad = run(input_grad_kernel, above, [line, line, model], row_count * depth * 16)
    small["ln1_gain", 0], small["ln1_shift", 0] = gain_sum, shift_sum
    block_out = run(
        functools.partial(block_out_kernel, top), entering + [out_bias, live], [model], row_count * depth * 4
    )[0]
    names = ("ln1_gain", "ln1_shift", "qv_bias", "proj_bias", "ln2_gain", "ln2_shift", "fc_bias", "out_bias")
    terms = [small[name, number] for name in names for number in range(top + 1)]
    flat = run(pack_kernel, terms, [(sum(term.shape[1] for term in terms) // LANES, LANES)], 1000, limit=SMALL)[0]
    scatter.flat = flat

    two, one = ((0, 1), (2,)), ((0, 1, 2),)
    first = scatter.fold(first)
    for _ in scatter.rest[1:]:
        scatter.step()
    scatter.launch(first, [flat, block_out], step=True)
    second = scatter.fold(first_chunks[2], out_chunk)
    first = scatter.fold(first, pieces=two)
    scatter.launch(second, ride=(first, 0))
    third = scatter.fold(fc_chunk)
    scatter.launch(third, ride=(first, 1))
    second = scatter.fold(second)
    scatter.launch(second)
    fourth = mix_chunk
    second = scatter.fold(second, pieces=two)
    scatter.launch(fourth, ride=(second, 0))
    third = scatter.fold(third)
    scatter.launch(third, ride=(second, 1), step=True)
    fourth, third = scatter.fold(fourth), scatter.fold(third, pieces=two)
    scatter.launch(fourth, ride=(third, 0), step=True)
    fourth = scatter.fold(fourth)
    scatter.rider = []
    scatter.launch(fourth, ride=(third, 1), step=True)
    fourth = scatter.fold(fourth, pieces=one)
    scatter.rider = []
    scatter.ride(fourth, 0)
    chunks = (first, second, third, fourth)

    layers = top + 1
    rows = depth // count
    sizes = [(layers, small[name, 0].shape[1]) for name in names]
    result = run(
        functools.partial(finish_kernel, [(chunk["parts"], chunk["pieces"]) for chunk in chunks], sizes),
        [keep for chunk in chunks for keep in chunk["keep"]] + [got for chunk in chunks for got in chunk["got"]] + [scatter.flat],
        [(layers, rows, hidden), (layers, rows, hidden), (layers, rows, width), (layers, 3, rows, width)] + sizes,
        1000,
    )
    out_sum, fc_sum, proj_sum, qkv_sum, *sums = result
    ln1_gain_sum, ln1_shift_sum, qv_bias_sum, proj_bias_sum, ln2_gain_sum, ln2_shift_sum, fc_bias_sum, out_bias_sum = sums
    return (
        block_out,
        input_grad,
        ln1_gain_sum,
        ln1_shift_sum,
        qkv_sum,
        qv_bias_sum.reshape(layers, 2, width),
        proj_sum.transpose(0, 2, 1),
        proj_bias_sum,
        ln2_gain_sum,
        ln2_shift_sum,
        fc_sum,
        fc_bias_sum,
        out_sum.transpose(0, 2, 1),
        out_bias_sum,
    )


def solution(mesh):
    in_specs = (
        P("dp", None),
        P("dp", None),
        P("dp", None),
        P("dp"),
        P(),
        P(),
        P(None, None, None, "tensor"),
        P(None, None, "tensor"),
        P(None, "tensor", None),
        P(),
        P(),
        P(),
        P(None, None, "tensor"),
        P(None, "tensor"),
        P(None, "tensor", None),
        P(),
    )
    out_specs = (
        P("dp", None),
        P("dp", None),
        P(),
        P(),
        P(None, None, "dp", "tensor"),
        P(None, None, "tensor"),
        P(None, "tensor", "dp"),
        P(),
        P(),
        P(),
        P(None, "dp", "tensor"),
        P(None, "tensor"),
        P(None, "tensor", "dp"),
        P(),
    )
    return jax.shard_map(
        functools.partial(on_device, mesh.shape["dp"], mesh.shape["tensor"]),
        mesh=mesh,
        in_specs=in_specs,
        out_specs=out_specs,
        check_vma=False,
    )
```

```python
import functools

import jax
import jax.numpy as jnp
from jax import lax
from jax.experimental import pallas as pl
from jax.experimental.pallas import tpu as pltpu
from jax.sharding import PartitionSpec as P

HEAD_DIM = 64
EPSILON = 1e-05
LANES = 128
HEAD_SCALE = HEAD_DIM ** (-0.5)
MASKED = -1e30
F32 = jnp.float32
BF16 = jnp.bfloat16
GELU_A = 0.7978845608028654
GELU_B = 0.044715
HIDDEN_TILE = 512
FLOWS = 3
LARGE = 24
LAST_SHARES = (4, 3, 2)
SMALL = 16
ROW_BLOCK = 384


def split_two(values):
    high = values.astype(BF16)
    return high, (values - high.astype(F32)).astype(BF16)


def product(left, right):
    return jnp.dot(left, right, preferred_element_type=F32)


def product_turned(left, right):
    return lax.dot_general(left, right, (((1,), (1,)), ((), ())), preferred_element_type=F32)


def turned_product(left, right):
    return lax.dot_general(left, right, (((0,), (0,)), ((), ())), preferred_element_type=F32)


def by_weight(pair, weight):
    return product(pair[0], weight) + product(pair[1], weight)


def by_weight_turned(pair, weight):
    return product_turned(pair[0], weight) + product_turned(pair[1], weight)


def normalize(values):
    centred = values - jnp.mean(values, axis=-1, keepdims=True)
    scale = lax.rsqrt(jnp.mean(centred * centred, axis=-1, keepdims=True) + EPSILON)
    return centred * scale, scale


def norm_backward(grad, unit, scale, norm_gain):
    gained = grad * norm_gain
    mean_grad = jnp.mean(gained, axis=-1, keepdims=True)
    mean_dot = jnp.mean(gained * unit, axis=-1, keepdims=True)
    return scale * (gained - mean_grad - unit * mean_dot)


def column_sum(values):
    return jnp.sum(values, axis=0, keepdims=True)


def gelu(values):
    bent = jnp.tanh(GELU_A * (values + GELU_B * values * values * values))
    return 0.5 * values * (1.0 + bent)


def gelu_slope(values):
    square = values * values
    bent = jnp.tanh(GELU_A * (values + GELU_B * values * square))
    inner = GELU_A * (1.0 + 3.0 * GELU_B * square)
    return 0.5 * (1.0 + bent) + 0.5 * values * (1.0 - bent * bent) * inner


def fill_mask(mask_ref, doc_ref, live_ref):
    shape = mask_ref.shape
    position = lax.broadcasted_iota(jnp.int32, (8, shape[1]), 1)
    documents = jnp.broadcast_to(doc_ref[...], (8, shape[1]))
    tags = jnp.where(position < live_ref[0], documents, -1).astype(F32)
    same = tags.T[:, :1] == tags[:1, :]
    causal = lax.broadcasted_iota(jnp.int32, shape, 1) <= lax.broadcasted_iota(jnp.int32, shape, 0)
    mask_ref[...] = jnp.where(same & causal, 1.0, 0.0)


def living(shape, live_ref):
    return jnp.where(lax.broadcasted_iota(jnp.int32, shape, 0) < live_ref[0], 1.0, 0.0)


def attend_kernel(number, first, *refs):
    if first:
        x_ref, *refs = refs
        values = x_ref[...]
    else:
        m_ref, part_ref, got_ref, out_bias_ref, *refs = refs
        values = m_ref[...] + (part_ref[...] + got_ref[...]) + out_bias_ref[number - 1:number, :]
    gain_ref, shift_ref, weight_ref, bias_ref, proj_ref, doc_ref, live_ref, *refs = refs
    if not first:
        x_out_ref, *refs = refs
        x_out_ref[...] = values
    normed_ref, qkv_ref, result_ref, logsum_ref, branch_ref, mask_ref = refs
    rows = values.shape[0]
    unit, _ = normalize(values)
    normed = unit * gain_ref[number:number + 1, :] + shift_ref[number:number + 1, :]
    normed_ref[...] = normed
    pair = split_two(normed)
    width = weight_ref.shape[-1]
    for member in range(3):
        piece = by_weight(pair, weight_ref[0, member])
        if member != 1:
            piece = piece + bias_ref[number, member // 2:member // 2 + 1, :]
        qkv_ref[:, member * width:(member + 1) * width] = piece
    fill_mask(mask_ref, doc_ref, live_ref)
    for head in range(width // HEAD_DIM):
        low_at = head * HEAD_DIM
        query, key, value = (
            split_two(qkv_ref[:, member * width + low_at:member * width + low_at + HEAD_DIM]) for member in range(3)
        )
        queries = jnp.concatenate([query[0], query[0], query[1]], axis=1)
        keys = jnp.concatenate([key[0], key[1], key[0]], axis=1)
        both = jnp.concatenate([value[0], value[1]], axis=1)
        for start in range(0, rows, ROW_BLOCK):
            stop = start + ROW_BLOCK
            scores = product_turned(queries[start:stop], keys[:stop]) * HEAD_SCALE
            scores = jnp.where(mask_ref[start:stop, :stop] > 0.5, scores, MASKED)
            peak = jnp.max(scores, axis=1, keepdims=True)
            weights = jnp.exp(scores - peak)
            total = jnp.sum(weights, axis=1, keepdims=True)
            logsum_ref[start:stop, head:head + 1] = peak + jnp.log(total)
            high, low = split_two(weights)
            mixed = product(high, both[:stop])
            mixed = mixed[:, :HEAD_DIM] + mixed[:, HEAD_DIM:] + product(low, value[0][:stop])
            result_ref[start:stop, low_at:low_at + HEAD_DIM] = mixed / total
    branch_ref[...] = by_weight(split_two(result_ref[...]), proj_ref[0])


def mlp_kernel(
    number, x_ref, part_ref, got_ref, proj_bias_ref, gain_ref, shift_ref, fc_ref, fc_bias_ref, out_ref,
    middle_ref, normed_ref, hidden_ref, active_ref, branch_ref,
):
    values = x_ref[...] + (part_ref[...] + got_ref[...]) + proj_bias_ref[number:number + 1, :]
    middle_ref[...] = values
    unit, _ = normalize(values)
    normed = unit * gain_ref[number:number + 1, :] + shift_ref[number:number + 1, :]
    normed_ref[...] = normed
    pair = split_two(normed)
    tiles = [slice(start, start + HIDDEN_TILE) for start in range(0, fc_ref.shape[-1], HIDDEN_TILE)]
    entered = lambda tile: by_weight(pair, fc_ref[0, :, tile]) + fc_bias_ref[number:number + 1, tile]
    total, hidden = None, entered(tiles[0])
    for at, tile in enumerate(tiles):
        later = entered(tiles[at + 1]) if at + 1 < len(tiles) else None
        active = gelu(hidden)
        term = by_weight(split_two(active), out_ref[0, tile, :])
        total = term if total is None else total + term
        hidden_ref[:, tile], active_ref[:, tile] = hidden, active
        hidden = later
    branch_ref[...] = total


def stream_grad(number, grad_ref, x_ref, part_ref, got_ref, gain_ref, gain_sum_ref, shift_sum_ref):
    unit, scale = normalize(x_ref[...])
    arriving = part_ref[...] + got_ref[...]
    gain_sum_ref[...] = column_sum(arriving * unit)
    shift_sum_ref[...] = column_sum(arriving)
    return grad_ref[...] + norm_backward(arriving, unit, scale, gain_ref[number:number + 1, :])


def mlp_back_kernel(number, top, *refs):
    if top:
        cotangent_ref, live_ref, *refs = refs
    else:
        above, refs = refs[:5], refs[5:]
    hidden_ref, fc_ref, out_ref, *refs = refs
    if top:
        grad = Masked(cotangent_ref, live_ref)[...]
    else:
        gain_sum_ref, shift_sum_ref, grad_ref, *refs = refs
        grad = stream_grad(number + 1, *above, gain_sum_ref, shift_sum_ref)
        grad_ref[...] = grad
    out_bias_ref, fc_bias_ref, hidden_grad_ref, branch_ref = refs
    out_bias_ref[...] = column_sum(grad)
    pair = split_two(grad)
    tiles = [slice(start, start + HIDDEN_TILE) for start in range(0, fc_ref.shape[-1], HIDDEN_TILE)]
    total, active_grad = None, by_weight_turned(pair, out_ref[0, tiles[0], :])
    for at, tile in enumerate(tiles):
        later = by_weight_turned(pair, out_ref[0, tiles[at + 1], :]) if at + 1 < len(tiles) else None
        hidden_grad = gelu_slope(hidden_ref[:, tile]) * active_grad
        active_grad = later
        hidden_grad_ref[:, tile] = hidden_grad
        fc_bias_ref[:, tile] = column_sum(hidden_grad)
        term = by_weight_turned(split_two(hidden_grad), fc_ref[0, :, tile])
        total = term if total is None else total + term
    branch_ref[...] = total


def attend_back_kernel(
    number, top, grad_ref, middle_ref, part_ref, got_ref, gain_ref, proj_ref, weight_ref, qkv_ref, result_ref, logsum_ref,
    doc_ref, live_ref,
    gain_sum_ref, shift_sum_ref, proj_bias_ref, bias_ref, middle_grad_ref, qkv_grad_ref, branch_ref,
    mask_ref, result_grad_ref,
):
    if top:
        grad_ref = Masked(grad_ref, live_ref)
    grad = stream_grad(number, grad_ref, middle_ref, part_ref, got_ref, gain_ref, gain_sum_ref, shift_sum_ref)
    middle_grad_ref[...] = grad
    proj_bias_ref[...] = column_sum(grad)
    result_grad_ref[...] = by_weight_turned(split_two(grad), proj_ref[0])
    fill_mask(mask_ref, doc_ref, live_ref)
    rows, width = result_ref.shape
    for head in range(width // HEAD_DIM):
        low_at = head * HEAD_DIM
        columns = slice(low_at, low_at + HEAD_DIM)
        query, key, value = (
            split_two(qkv_ref[:, member * width + low_at:member * width + low_at + HEAD_DIM]) for member in range(3)
        )
        given = result_grad_ref[:, columns]
        given_pair = split_two(given)
        delta = jnp.sum(given * result_ref[:, columns], axis=1, keepdims=True)
        queries = jnp.concatenate([query[0], query[0], query[1]], axis=1)
        keys = jnp.concatenate([key[0], key[1], key[0]], axis=1)
        givens = jnp.concatenate([given_pair[0], given_pair[0], given_pair[1]], axis=1)
        values = jnp.concatenate([value[0], value[1], value[0]], axis=1)
        key_both = jnp.concatenate([key[0], key[1]], axis=1)
        query_both = jnp.concatenate([query[0], query[1]], axis=1)
        given_both = jnp.concatenate([given_pair[0], given_pair[1]], axis=1)
        for start in range(0, rows, ROW_BLOCK):
            stop = start + ROW_BLOCK
            scores = product_turned(queries[start:stop], keys[:stop]) * HEAD_SCALE
            scores = jnp.where(mask_ref[start:stop, :stop] > 0.5, scores, MASKED)
            weights = jnp.exp(scores - logsum_ref[start:stop, head:head + 1])
            weights_grad = product_turned(givens[start:stop], values[:stop])
            scores_grad = weights * (weights_grad - delta[start:stop]) * HEAD_SCALE
            high, low = split_two(scores_grad)
            mixed = product(high, key_both[:stop])
            qkv_grad_ref[start:stop, columns] = (
                mixed[:, :HEAD_DIM] + mixed[:, HEAD_DIM:] + product(low, key[0][:stop])
            )
            mixed = turned_product(high, query_both[start:stop])
            key_grad = mixed[:, :HEAD_DIM] + mixed[:, HEAD_DIM:] + turned_product(low, query[0][start:stop])
            high, low = split_two(weights)
            mixed = turned_product(high, given_both[start:stop])
            value_grad = mixed[:, :HEAD_DIM] + mixed[:, HEAD_DIM:] + turned_product(low, given_pair[0][start:stop])
            for member, term in ((1, key_grad), (2, value_grad)):
                at = slice(member * width + low_at, member * width + low_at + HEAD_DIM)
                if start == 0:
                    qkv_grad_ref[:stop, at] = term
                else:
                    qkv_grad_ref[:start, at] += term[:start]
                    qkv_grad_ref[start:stop, at] = term[start:]
    total = None
    for member in range(3):
        piece = qkv_grad_ref[:, member * width:(member + 1) * width]
        if member != 1:
            bias_ref[:, (member // 2) * width:(member // 2 + 1) * width] = column_sum(piece)
        term = by_weight_turned(split_two(piece), weight_ref[0, member])
        total = term if total is None else total + term
    branch_ref[...] = total


def input_grad_kernel(grad_ref, x_ref, part_ref, got_ref, gain_ref, gain_sum_ref, shift_sum_ref, out_ref):
    out_ref[...] = stream_grad(0, grad_ref, x_ref, part_ref, got_ref, gain_ref, gain_sum_ref, shift_sum_ref)


def block_out_kernel(number, middle_ref, part_ref, got_ref, out_bias_ref, live_ref, out_ref):
    values = middle_ref[...] + (part_ref[...] + got_ref[...]) + out_bias_ref[number:number + 1, :]
    out_ref[...] = values * living(values.shape, live_ref)


def whole():
    return pl.BlockSpec(memory_space=pltpu.VMEM)


class Fetched:
    def __init__(self, source, target, semaphore):
        self.copy = pltpu.make_async_copy(source, target, semaphore)
        self.copy.start()
        self.target = target
        self.shape = target.shape
        self.waiting = True

    def __getitem__(self, index):
        if self.waiting:
            self.copy.wait()
            self.waiting = False
        return self.target[index]


class Masked:
    def __init__(self, ref, live_ref):
        self.ref, self.live_ref, self.shape = ref, live_ref, ref.shape

    def __getitem__(self, index):
        return self.ref[index] * living(self.shape, self.live_ref)


class Saved:
    def __init__(self, target, stage, semaphores, late):
        self.target, self.stage, self.semaphores, self.late = target, stage, semaphores, late
        self.shape, self.copies = stage.shape, []

    def push(self, index):
        source, target = self.stage.at[index], self.target.at[index]
        self.copies.append(pltpu.make_async_copy(source, target, self.semaphores.at[len(self.copies)]))
        self.copies[-1].start()

    def __getitem__(self, index):
        return self.stage[index]

    def __setitem__(self, index, values):
        self.stage[index] = values
        if not self.late:
            self.push(index)

    def finish(self):
        if self.late:
            self.push(Ellipsis)
        for copy in self.copies:
            copy.wait()


class Halves:
    def __init__(self, upper, lower):
        self.refs = upper, lower

    def __getitem__(self, index):
        return jnp.concatenate([ref[...] for ref in self.refs], axis=0)

    def __setitem__(self, index, values):
        rows = values.shape[0] // 2
        self.refs[0][...], self.refs[1][...] = values[:rows], values[rows:]


def wrapped(kernel, operand_kinds, out_kinds, owned, *refs):
    refs = list(refs)
    mine, refs = refs[len(refs) - owned:], refs[:len(refs) - owned]
    made, saved = [], []
    for kind, detail in operand_kinds + out_kinds:
        if kind == "halves":
            made.append(Halves(refs.pop(0), refs.pop(0)))
        elif kind == "layer":
            made.append(Fetched(refs.pop(0).at[pl.ds(detail, 1)], mine.pop(0), mine.pop(0)))
        elif kind == "stored":
            made.append(Fetched(refs.pop(0), mine.pop(0), mine.pop(0)))
        elif kind == "saved":
            made.append(Saved(refs.pop(0), mine.pop(0), mine.pop(0), detail))
            saved.append(made[-1])
        else:
            made.append(refs.pop(0))
    kernel(*made, *refs)
    for out in saved:
        out.finish()


class Stored:
    def __init__(self, array):
        self.array = array


class Save:
    def __init__(self, shape, late=False):
        self.shape, self.late = shape, late


class Scalar:
    def __init__(self, array):
        self.array = array


SAVED_PIECES = 4


def run(kernel, operands, outs, flops, scratch=(), limit=LARGE):
    hbm = pltpu.MemorySpace.HBM
    specs, arrays, kinds, owned = [], [], [], []
    for operand in operands:
        if isinstance(operand, (tuple, Stored)):
            if isinstance(operand, Stored):
                array, number, shape = operand.array, None, operand.array.shape
                kinds.append(("stored", None))
            else:
                array, number = operand
                shape = (1,) + array.shape[1:]
                kinds.append(("layer", number))
            specs.append(pl.BlockSpec(memory_space=hbm))
            owned += [pltpu.VMEM(shape, array.dtype), pltpu.SemaphoreType.DMA(())]
            arrays.append(pltpu.with_memory_space_constraint(array, hbm))
        elif isinstance(operand, Scalar):
            kinds.append(("scalar", None))
            specs.append(pl.BlockSpec(memory_space=pltpu.SMEM))
            arrays.append(operand.array)
        elif isinstance(operand, list):
            kinds.append(("halves", None))
            specs += [whole()] * 2
            arrays += operand
        else:
            kinds.append(("whole", None))
            specs.append(whole())
            arrays.append(operand)
    shapes, out_kinds, out_specs = [], [], []
    for out in outs:
        if isinstance(out, list):
            out_kinds.append(("halves", None))
            shapes += [jax.ShapeDtypeStruct((out[0][0] // 2, out[0][1]), F32)] * 2
            out_specs += [whole()] * 2
        elif isinstance(out, Save):
            out_kinds.append(("saved", out.late))
            shapes.append(pltpu.MemorySpace.HBM(out.shape, F32))
            out_specs.append(pl.BlockSpec(memory_space=hbm))
            owned += [pltpu.VMEM(out.shape, F32), pltpu.SemaphoreType.DMA((SAVED_PIECES,))]
        else:
            out_kinds.append(("whole", None))
            shapes.append(jax.ShapeDtypeStruct(out, F32))
            out_specs.append(whole())
    results = list(
        pl.pallas_call(
            functools.partial(wrapped, kernel, kinds, out_kinds, len(owned)),
            out_shape=shapes,
            in_specs=specs,
            out_specs=out_specs,
            scratch_shapes=list(scratch) + owned,
            compiler_params=pltpu.CompilerParams(vmem_limit_bytes=limit * 2**20),
            cost_estimate=pl.CostEstimate(flops=flops, bytes_accessed=10**5, transcendentals=0),
        )(*arrays)
    )
    return [[results.pop(0), results.pop(0)] if kind == "halves" else results.pop(0) for kind, _ in out_kinds]


def bit_orders(count):
    bits = [1 << at for at in range(count.bit_length() - 1)]
    lead, rest = bits[:FLOWS], bits[FLOWS:]
    return [lead[at:] + lead[:at] for at in range(FLOWS)], rest


def block_masks(order):
    masks = [0]
    for bit in reversed(order):
        masks = masks + [mask + bit for mask in masks]
    return masks


def grad_kernel(mask_lists, permuted, pairs, top, halves, me_ref, live_ref, *refs):
    ins, refs = refs[: 2 * len(pairs)], refs[2 * len(pairs):]
    outs, (turned_high, turned_low, high_ref, low_ref) = refs[: len(halves) * FLOWS], refs[len(halves) * FLOWS:]
    depth = high_ref.shape[0]
    half = depth // 2
    starts = [0] * FLOWS
    for at, widths in enumerate(pairs):
        a_ref, b_ref = ins[2 * at], ins[2 * at + 1]
        if top:
            a_ref = Masked(a_ref, live_ref)
        if not permuted:
            turned_high[...], turned_low[...] = split_two(a_ref[...].T)
        for flow, masks in enumerate(mask_lists):
            if permuted:
                high_ref[...], low_ref[...] = split_two(a_ref[flow])
            else:
                rows = depth // len(masks)
                for place, mask in enumerate(masks):
                    if place // (len(masks) // 2) not in halves:
                        continue
                    source = pl.ds(pl.multiple_of((me_ref[0] ^ mask) * rows, 16), rows)
                    target = pl.ds(place * rows, rows)
                    high_ref[target, :] = turned_high[source, :]
                    low_ref[target, :] = turned_low[source, :]
            start, width, column = starts[flow], widths[flow], sum(widths[:flow])
            part_high, part_low = split_two(b_ref[:, column:column + width])
            for place, which in enumerate(halves):
                rows_at = pl.ds(which * half, half)
                outs[len(halves) * flow + place][:, start:start + width] = (
                    product(high_ref[rows_at, :], part_high)
                    + product(high_ref[rows_at, :], part_low)
                    + product(low_ref[rows_at, :], part_high)
                )
            starts[flow] += width


def flow_widths(columns, shares):
    tiles = columns // LANES
    return tuple(LANES * (tiles * share // sum(shares)) for share in shares)


def grad_parts(pairs, names, me, live, count, top=False, shares=(1,) * FLOWS, sends_first=False):
    orders, rest = bit_orders(count)
    mask_lists = [block_masks(order + rest) for order in orders]
    bare = [[one.array if isinstance(one, Stored) else one for one in two] for two in pairs]
    tokens, depth = bare[0][0].shape
    rows = depth // count
    permuted = rows % 16 != 0
    operands, widths = [Scalar(me.reshape(1)), Scalar(live)], []
    for (left, right), (left_array, right_array) in zip(pairs, bare):
        if permuted:
            if top:
                left_array = jnp.where(jnp.arange(tokens)[:, None] < live[0], left_array, 0.0)
            blocks = left_array.T.reshape(count, rows, tokens)
            left = jnp.stack(
                [jnp.take(blocks, me ^ jnp.array(masks, jnp.int32), axis=0).reshape(depth, tokens) for masks in mask_lists]
            )
        operands += [left, right]
        widths.append(flow_widths(right_array.shape[1], shares))
    def halves_of(*halves):
        outs = [(depth // 2, sum(one[flow] for one in widths)) for flow in range(FLOWS) for _ in halves]
        kernel = functools.partial(grad_kernel, mask_lists, permuted, widths, top and not permuted, halves)
        return run(kernel, operands, outs, 10**6, [pltpu.VMEM((depth, tokens), BF16)] * 4)

    if sends_first:
        sends, keeps = halves_of(1), halves_of(0)
    else:
        both = halves_of(1, 0)
        sends, keeps = both[0::2], both[1::2]
    return {"send": sends, "keep": keeps, "phase": 0, "parts": list(zip(names, widths))}


def fold_kernel(pieces, members, *refs):
    gots, keeps, outs = refs[: FLOWS * members], refs[FLOWS * members : 2 * FLOWS * members], refs[2 * FLOWS * members :]
    half = gots[0].shape[0] // 2
    for number, piece in enumerate(pieces):
        at = 0
        for flow in piece:
            for member in range(members):
                got, keep = gots[FLOWS * member + flow], keeps[FLOWS * member + flow]
                columns = slice(at, at + got.shape[1])
                at += got.shape[1]
                for which in (1, 0):
                    rows = slice(which * half, (which + 1) * half)
                    outs[len(pieces) * (1 - which) + number][:, columns] = got[rows, :] + keep[rows, :]


class Scatter:
    def __init__(self, count):
        self.count = count
        self.orders, self.rest = bit_orders(count)
        self.axes = [order[0] for order in self.orders]
        self.before, self.last = [], []
        self.rider = []
        self.flat, self.steps = None, self.rest + sorted(self.axes)

    def swap(self, values, bit):
        return lax.ppermute(values, "dp", [(one, one ^ bit) for one in range(self.count)])

    def launch(self, chunk, tokens=(), ride=None, step=False, early=False):
        gots, arrived = [None] * FLOWS, []
        for axis, bit in enumerate(self.axes):
            flow = [order[chunk["phase"]] for order in self.orders].index(bit)
            waits = list(tokens) + self.before
            if early and axis == FLOWS - 1:
                (send,) = after([chunk["send"][flow]], waits)
                gots[flow] = self.swap(send, bit)
                arrived.append(gots[flow])
                continue
            waits += self.rider
            if self.last:
                waits.append(self.last[axis])
            (send,) = after([chunk["send"][flow]], waits)
            gots[flow] = self.swap(send, bit)
            arrived.append(gots[flow])
        chunk["got"] = gots
        if ride:
            self.ride(*ride)
        if step:
            self.rider = self.rider + [self.step()]
        self.before, self.last = self.last, arrived

    def step(self):
        (send,) = after([self.flat], self.last)
        got = self.swap(send, self.steps.pop(0))
        self.flat = self.flat + got
        return got

    def ride(self, chunk, piece):
        (send,), keep = after([chunk["send"][piece]], self.before + self.rider), chunk["keep"][piece]
        for bit in self.rest[:-1]:
            total = keep + self.swap(send, bit)
            half = total.shape[0] // 2
            keep, send = total[:half], total[half:]
        got = self.swap(send, self.rest[-1])
        chunk["keep"][piece], chunk["got"][piece] = keep, got
        self.rider = [got]

    def fold(self, *chunks, pieces=tuple((flow,) for flow in range(FLOWS))):
        rows = chunks[0]["got"][0].shape[0]
        widths = [sum(chunk["got"][flow].shape[1] for chunk in chunks) for flow in range(FLOWS)]
        outs = [(rows // 2, sum(widths[flow] for flow in piece)) for piece in pieces] * 2
        operands = [got for chunk in chunks for got in chunk["got"]] + [keep for chunk in chunks for keep in chunk["keep"]]
        result = run(functools.partial(fold_kernel, pieces, len(chunks)), operands, outs, rows * sum(widths), limit=SMALL)
        return {
            "parts": [part for chunk in chunks for part in chunk["parts"]],
            "phase": chunks[0]["phase"] + 1,
            "pieces": pieces,
            "send": result[:len(pieces)],
            "keep": result[len(pieces):],
            "got": [None] * len(pieces),
        }


def pack_kernel(*refs):
    *terms, out_ref = refs
    at = 0
    for term in terms:
        for start in range(0, term.shape[1], LANES):
            out_ref[at:at + 1, :] = term[:, start:start + LANES]
            at += 1


def finish_kernel(layout, small, *refs):
    pairs = sum(len(pieces) for _, pieces in layout)
    keeps, gots, small_ref = refs[:pairs], refs[pairs:2 * pairs], refs[2 * pairs]
    out_ref, fc_ref, proj_ref, qkv_ref, *small_refs = refs[2 * pairs + 1:]
    number = 0
    for parts, pieces in layout:
        for piece in pieces:
            total = keeps[number][...] + gots[number][...]
            number += 1
            at = 0
            for flow in piece:
                for (name, layer), widths in parts:
                    column = sum(widths[:flow])
                    for start in range(0, widths[flow], LANES):
                        block = total[:, at + start:at + start + LANES]
                        member, place = divmod(column + start, qkv_ref.shape[-1])
                        if name == "qkv":
                            qkv_ref[layer, member, :, place:place + LANES] = block
                        else:
                            ref = {"out": out_ref, "fc": fc_ref, "proj": proj_ref}[name]
                            ref[layer, :, column + start:column + start + LANES] = block
                    at += widths[flow]
    at = 0
    for ref, (layers, size) in zip(small_refs, small):
        for layer in range(layers):
            for start in range(0, size, LANES):
                ref[layer:layer + 1, start:start + LANES] = small_ref[at:at + 1, :]
                at += 1


def after(values, tokens):
    if not tokens:
        return values
    return lax.optimization_barrier((values, list(tokens)))[0]


def on_device(
    count,
    pair,
    tokens,
    cotangent,
    doc_ids,
    live_rows,
    ln1_gain,
    ln1_shift,
    qkv_weight,
    qv_bias,
    proj_weight,
    proj_bias,
    ln2_gain,
    ln2_shift,
    fc_weight,
    fc_bias,
    out_weight,
    out_bias,
):
    row_count, depth = tokens.shape
    width, hidden = qkv_weight.shape[-1], fc_weight.shape[-1]
    top = qkv_weight.shape[0] - 1
    me = lax.axis_index("dp").astype(jnp.int32)
    model, half, wide, line = (row_count, depth), (row_count, width), (row_count, hidden), (1, depth)
    mask_scratch = pltpu.VMEM((row_count, row_count), F32)
    macs = row_count * depth * hidden
    live = Scalar(live_rows)
    groups = [Stored(doc_ids), live]
    ln1_gain, ln1_shift, ln2_gain, ln2_shift = Stored(ln1_gain), Stored(ln1_shift), Stored(ln2_gain), Stored(ln2_shift)
    qv_bias, proj_bias, fc_bias, out_bias = Stored(qv_bias), Stored(proj_bias), Stored(fc_bias), Stored(out_bias)

    def exchange(halves):
        return [lax.ppermute(part, "tensor", [(one, one ^ 1) for one in range(pair)]) for part in halves]

    stored = []
    entering = [Stored(tokens)]
    for number in range(top + 1):
        first = number == 0
        outs = [] if first else [Save(model)]
        outs += [Save(model), Save((row_count, 3 * width)), half, (row_count, LANES), [model]]
        result = run(
            functools.partial(attend_kernel, number, first),
            entering + ([] if first else [out_bias])
            + [ln1_gain, ln1_shift, (qkv_weight, number), qv_bias, (proj_weight, number)] + groups,
            outs, 8 * macs, [mask_scratch],
        )
        stream = Stored(tokens if first else result[0])
        normed, qkv, mixed, logsum, branch = result[-5:]
        middle, normed_two, hidden_in, active, branch_two = run(
            functools.partial(mlp_kernel, number),
            [stream, branch, exchange(branch), proj_bias, ln2_gain, ln2_shift, (fc_weight, number), fc_bias, (out_weight, number)],
            [Save(model), Save(model), Save(wide), Save(wide), [model]], 8 * macs,
        )
        entering = [Stored(middle), branch_two, exchange(branch_two)]
        kept = [Stored(array) for array in (normed, qkv, middle, normed_two, hidden_in, active)]
        stored.append((stream, *kept[:2], mixed, logsum, *kept[2:]))

    scatter = Scatter(count)
    small = {}

    def mlp_back(number, operands, hidden_in):
        is_top = number == top
        outs = [] if is_top else [line, line, model]
        result = run(
            functools.partial(mlp_back_kernel, number, is_top),
            operands + [hidden_in, (fc_weight, number), (out_weight, number)],
            outs + [line, (1, hidden), wide, [model]], 24 * macs,
        )
        if is_top:
            grad = Stored(cotangent)
        else:
            small["ln1_gain", number + 1], small["ln1_shift", number + 1], grad = result[:3]
        small["out_bias", number], small["fc_bias", number], hidden_grad, branch = result[-4:]
        return grad, hidden_grad, branch

    def attend_back(number, grad, branch, got):
        stream, normed, qkv, mixed, logsum, middle = stored[number][:6]
        result = run(
            functools.partial(attend_back_kernel, number, number == top),
            [grad, middle, branch, got, ln2_gain, (proj_weight, number), (qkv_weight, number), qkv, mixed, logsum] + groups,
            [line, line, line, (1, 2 * width), model, (row_count, 3 * width), [model]], 32 * macs,
            [mask_scratch, pltpu.VMEM(half, F32)],
        )
        (small["ln2_gain", number], small["ln2_shift", number], small["proj_bias", number], small["qv_bias", number]) = result[:4]
        return result[4:]

    def out_parts(number, grad):
        return grad_parts([(grad, stored[number][8])], [("out", number)], me, live_rows, count, number == top, sends_first=number == top)

    def fc_pair(number, hidden_grad):
        return (stored[number][6], hidden_grad), ("fc", number)

    def proj_pair(number, middle_grad):
        return (middle_grad, stored[number][3]), ("proj", number)

    def qkv_pair(number, qkv_grad):
        return (stored[number][1], qkv_grad), ("qkv", number)

    def parts_of(*named, **options):
        return grad_parts([pair for pair, _ in named], [name for _, name in named], me, live_rows, count, **options)

    grad, first_chunks = Stored(cotangent), None
    for number in reversed(range(top + 1)):
        if number == top:
            out_chunk = out_parts(number, grad)
            scatter.launch(out_chunk)
            (hidden_in,) = after([stored[number][7].array], out_chunk["send"][:1])
            grad, hidden_grad, branch = mlp_back(number, [grad, live], Stored(hidden_in))
            got = exchange(branch)
            fc_chunk = parts_of(fc_pair(number, hidden_grad))
            scatter.launch(fc_chunk)
        else:
            above[:1] = after(above[:1], scatter.before)
            grad, hidden_grad, branch = mlp_back(number, above, stored[number][7])
            got = exchange(branch)
            out_chunk = out_parts(number, grad)
            scatter.launch(out_chunk, branch)
        got = after(got, scatter.before)
        middle_grad, qkv_grad, branch = attend_back(number, grad, branch, got)
        got = exchange(branch)
        if number == top:
            mix_chunk = parts_of(proj_pair(number, middle_grad), qkv_pair(number, qkv_grad), sends_first=True)
            scatter.launch(mix_chunk)
            first_chunks = out_chunk, fc_chunk, mix_chunk
        else:
            first = scatter.fold(*first_chunks[:2])
            scatter.launch(first, branch)
            fc_chunk = parts_of(fc_pair(number, hidden_grad), proj_pair(number, middle_grad))
            scatter.launch(fc_chunk, first_chunks[2]["keep"][:1])
            mix_chunk = parts_of(qkv_pair(number, qkv_grad), shares=LAST_SHARES)
        above = [middle_grad, stored[number][0], branch, got, ln1_gain]
    gain_sum, shift_sum, input_grad = run(input_grad_kernel, above, [line, line, model], row_count * depth * 16)
    small["ln1_gain", 0], small["ln1_shift", 0] = gain_sum, shift_sum
    block_out = run(
        functools.partial(block_out_kernel, top), entering + [out_bias, live], [model], row_count * depth * 4
    )[0]
    names = ("ln1_gain", "ln1_shift", "qv_bias", "proj_bias", "ln2_gain", "ln2_shift", "fc_bias", "out_bias")
    terms = [small[name, number] for name in names for number in range(top + 1)]
    flat = run(pack_kernel, terms, [(sum(term.shape[1] for term in terms) // LANES, LANES)], 1000, limit=SMALL)[0]
    scatter.flat = flat

    two, one = ((0, 1), (2,)), ((0, 1, 2),)
    first = scatter.fold(first)
    for _ in scatter.rest[1:]:
        scatter.step()
    scatter.launch(first, [flat, block_out], step=True)
    second = scatter.fold(first_chunks[2], out_chunk)
    first = scatter.fold(first, pieces=two)
    scatter.launch(second, ride=(first, 0))
    third = scatter.fold(fc_chunk)
    scatter.launch(third, ride=(first, 1))
    second = scatter.fold(second)
    scatter.launch(second)
    fourth = mix_chunk
    second = scatter.fold(second, pieces=two)
    scatter.launch(fourth, ride=(second, 0))
    third = scatter.fold(third)
    scatter.launch(third, ride=(second, 1), step=True)
    fourth, third = scatter.fold(fourth), scatter.fold(third, pieces=two)
    scatter.launch(fourth, ride=(third, 0), step=True)
    fourth = scatter.fold(fourth)
    scatter.rider = []
    scatter.launch(fourth, ride=(third, 1), step=True)
    fourth = scatter.fold(fourth, pieces=one)
    scatter.rider = []
    scatter.ride(fourth, 0)
    chunks = (first, second, third, fourth)

    layers = top + 1
    rows = depth // count
    sizes = [(layers, small[name, 0].shape[1]) for name in names]
    result = run(
        functools.partial(finish_kernel, [(chunk["parts"], chunk["pieces"]) for chunk in chunks], sizes),
        [keep for chunk in chunks for keep in chunk["keep"]] + [got for chunk in chunks for got in chunk["got"]] + [scatter.flat],
        [(layers, rows, hidden), (layers, rows, hidden), (layers, rows, width), (layers, 3, rows, width)] + sizes,
        1000,
    )
    out_sum, fc_sum, proj_sum, qkv_sum, *sums = result
    ln1_gain_sum, ln1_shift_sum, qv_bias_sum, proj_bias_sum, ln2_gain_sum, ln2_shift_sum, fc_bias_sum, out_bias_sum = sums
    return (
        block_out,
        input_grad,
        ln1_gain_sum,
        ln1_shift_sum,
        qkv_sum,
        qv_bias_sum.reshape(layers, 2, width),
        proj_sum.transpose(0, 2, 1),
        proj_bias_sum,
        ln2_gain_sum,
        ln2_shift_sum,
        fc_sum,
        fc_bias_sum,
        out_sum.transpose(0, 2, 1),
        out_bias_sum,
    )


def solution(mesh):
    in_specs = (
        P("dp", None),
        P("dp", None),
        P("dp", None),
        P("dp"),
        P(),
        P(),
        P(None, None, None, "tensor"),
        P(None, None, "tensor"),
        P(None, "tensor", None),
        P(),
        P(),
        P(),
        P(None, None, "tensor"),
        P(None, "tensor"),
        P(None, "tensor", None),
        P(),
    )
    out_specs = (
        P("dp", None),
        P("dp", None),
        P(),
        P(),
        P(None, None, "dp", "tensor"),
        P(None, None, "tensor"),
        P(None, "tensor", "dp"),
        P(),
        P(),
        P(),
        P(None, "dp", "tensor"),
        P(None, "tensor"),
        P(None, "tensor", "dp"),
        P(),
    )
    return jax.shard_map(
        functools.partial(on_device, mesh.shape["dp"], mesh.shape["tensor"]),
        mesh=mesh,
        in_specs=in_specs,
        out_specs=out_specs,
        check_vma=False,
    )
```
